256 devices in a mesh: seq: 128 (over y, z, x), head: 2 (over core).
Axes of the slice: x: 4, y: 4, z: 8, core: 2. Of those that a mesh axis runs over, the one named last changes fastest.
Arguments:
- queries: bfloat16 [256, 73728], P('seq', 'head'), may hold values from -6 to 6
- cache: bfloat16 [16, 1024, 36864], P(None, 'seq'), may hold values from -6 to 6
- selected: int32 [256, 32], replicated, may hold values from 0 to 1023, as said below
Outputs:
- attended: bfloat16 [256, 65536], P('seq')
The draws below stay inside these ranges and needn't reach their ends.
Inputs may be any that keep to these rules, and one draw needn't show every extreme that they name: `selected`: the 32 entries of one row are different blocks. The entries of the 2 rows on one index of seq (aligned runs of 2 rows) hold together at most 1 block of any range of 8 consecutive blocks starting at a multiple of 8, and exactly 1 of some range.
All inputs are finite; a program needn't handle non-finite values.
Results may differ from the reference program's by a relative error of at most 0.004.
Values may be sent and summed in bfloat16 or wider, within the bound.
No kernel may reach another device: no remote copies, remote signals or barrier semaphores. Data moves between devices by JAX's collectives and lax.ppermute only.
A program may use at most 192 MiB of HBM per device.

```python
import jax
import jax.numpy as jnp
from jax import lax

H = 128
KL = 512
KR = 64
BLOCK = 64
TOPK = 32
REQUESTS = 16
STEPS = 8
DRAFTS = 2
BLK_DEV = 8
ROWS = 256
RDEV = 2
NBLK = 1024


def draw_cache(key, part):
    key = jax.random.fold_in(key, 11)
    base_key = jax.random.fold_in(key, 0)
    shape = (REQUESTS, NBLK, BLOCK, KL + KR)
    values = jnp.clip(jax.random.normal(base_key, shape, jnp.float32), -6.0, 6.0)
    return values.reshape(REQUESTS, NBLK, BLOCK * (KL + KR)).astype(jnp.bfloat16)


def draw_queries(key, part):
    key = jax.random.fold_in(key, 23)
    base_key = jax.random.fold_in(key, 0)
    shape = (ROWS, H, KL + KR)
    values = jnp.clip(1.2 * jax.random.normal(base_key, shape, jnp.float32), -6.0, 6.0)
    return values.reshape(ROWS, H * (KL + KR)).astype(jnp.bfloat16)


def draw_selected(key, part):
    key = jax.random.fold_in(key, 37)
    perm_key, shift_key, inner_key = jax.random.split(key, 3)
    ranges = NBLK // BLK_DEV
    device_groups = ROWS // RDEV
    perm_scores = jax.random.randint(perm_key, (device_groups, ranges), 0, 1 << 16, dtype=jnp.int32) * ranges + jnp.arange(ranges, dtype=jnp.int32)
    range_perm = jnp.argsort(perm_scores, axis=-1, stable=True).astype(jnp.int32)
    shifts = jax.random.randint(shift_key, (device_groups, 1, 1), 0, ranges, dtype=jnp.int32)
    row_ids = jnp.arange(RDEV, dtype=jnp.int32)[None, :, None]
    pick_ids = jnp.arange(TOPK, dtype=jnp.int32)[None, None, :]
    position = (row_ids * TOPK + pick_ids + shifts) % ranges
    position = jnp.broadcast_to(position, (device_groups, RDEV, TOPK))
    spread_perm = jnp.broadcast_to(range_perm[:, None, :], (device_groups, RDEV, ranges))
    chosen_range = jnp.take_along_axis(spread_perm, position, axis=-1).astype(jnp.int32).reshape(ROWS, TOPK)
    occurrence = jnp.broadcast_to(jnp.arange(TOPK, dtype=jnp.int32)[None, :] // ranges, (ROWS, TOPK))
    inner_scores = jax.random.randint(inner_key, (ROWS, ranges, BLK_DEV), 0, 1 << 16, dtype=jnp.int32) * BLK_DEV + jnp.arange(BLK_DEV, dtype=jnp.int32)
    inner_perm = jnp.argsort(inner_scores, axis=-1, stable=True).astype(jnp.int32).reshape(ROWS, ranges * BLK_DEV)
    inner = jnp.take_along_axis(inner_perm, chosen_range * BLK_DEV + occurrence, axis=-1).astype(jnp.int32)
    return (chosen_range * BLK_DEV + inner).astype(jnp.int32)


def setup_inputs(seed: int = 0) -> dict:
    keys = jax.random.split(jax.random.key(seed), 4)
    queries = draw_queries(jax.random.fold_in(keys[3], 71), 0)
    cache = draw_cache(jax.random.fold_in(keys[3], 71), 0)
    selected = draw_selected(jax.random.fold_in(keys[3], 71), 0)
    return dict(queries=queries, cache=cache, selected=selected)


score_scale = 192.0 ** -0.5


def reference(queries, cache, selected):
    row_span = STEPS * DRAFTS
    feature_width = KL + KR
    block_rows = cache.reshape(REQUESTS * NBLK, BLOCK, feature_width)

    def attend_row(row_index):
        request = row_index // row_span
        picked = lax.dynamic_index_in_dim(selected, row_index, 0, keepdims=False)
        flat_blocks = (request * NBLK + picked).astype(jnp.int32)
        key_rows = jnp.take(block_rows, flat_blocks, axis=0)
        query_rows = lax.dynamic_index_in_dim(queries, row_index, 0, keepdims=False).reshape(H, feature_width)
        scores = jnp.einsum("hk,btk->hbt", query_rows.astype(jnp.float32), key_rows.astype(jnp.float32)) * score_scale
        block_top = jnp.max(scores, axis=-1)
        weights = jnp.exp(scores - block_top[:, :, None])
        block_total = jnp.sum(weights, axis=-1)
        rounded = weights.astype(jnp.bfloat16)
        values = key_rows[:, :, :KL].astype(jnp.float32)
        block_out = jnp.einsum("hbt,btv->hbv", rounded.astype(jnp.float32), values)
        peak = jnp.max(block_top, axis=1, keepdims=True)
        factor = jnp.exp(block_top - peak)
        numerator = jnp.sum(factor[:, :, None] * block_out, axis=1)
        denominator = jnp.sum(factor * block_total, axis=1)
        output = numerator / denominator[:, None]
        return output.astype(jnp.bfloat16).reshape(H * KL)

    return lax.map(attend_row, jnp.arange(ROWS, dtype=jnp.int32))
```

```python
import functools

import jax
import jax.numpy as jnp
from jax import lax
from jax.experimental import pallas as pl
from jax.experimental.pallas import tpu as pltpu
from jax.sharding import Mesh
from jax.sharding import PartitionSpec as P

KL = 512
KR = 64
FEAT = KL + KR
WIDE = KL + 2 * KR
BLOCK = 64
PAIRS = BLOCK // 2
PAIR_WIDTH = 2 * FEAT
TOPK = 32
RDEV = 2
BLK_DEV = 8
HEADS = 64
NY, NZ, NX = 4, 8, 4
PLANE = NY * NX
SEQ = NY * NZ * NX
ROWS_LOCAL = RDEV * HEADS
TAIL = 16
EMPTY = -1e30

score_scale = 192.0 ** (-0.5)

OFFSETS = (((4, 6), (3, 5)), ((2, 0), (1, 7)))

VMEM_LIMIT = 48 * 1024 * 1024


def pick_kernel(zd_ref, inner_ref, cache_ref, out_ref):
    base = (pl.program_id(1) * NZ + zd_ref[pl.program_id(0)]) * NX
    row = lax.broadcasted_iota(jnp.int32, (NX * PAIRS, BLK_DEV * PAIRS), 0)
    col = lax.broadcasted_iota(jnp.int32, (NX * PAIRS, BLK_DEV * PAIRS), 1)
    owner = row >> 5
    block = jnp.full(row.shape, inner_ref[base], jnp.int32)
    for i in range(1, NX):
        block = jnp.where(owner == i, inner_ref[base + i], block)
    hit = ((col >> 3) == (row & (PAIRS - 1))) & ((col & (BLK_DEV - 1)) == block)
    onehot = jnp.where(hit, 1.0, 0.0).astype(jnp.bfloat16)
    pieces = [
        cache_ref[0, :, p * PAIR_WIDTH : (p + 1) * PAIR_WIDTH].astype(jnp.float32)
        for p in range(PAIRS)
    ]
    stacked = jnp.concatenate(pieces, axis=0).astype(jnp.bfloat16)
    picked = jnp.dot(onehot, stacked, preferred_element_type=jnp.float32)
    out_ref[0, :, 0] = picked.astype(jnp.bfloat16).reshape(NX, PAIRS, PAIR_WIDTH)


def pick_blocks(zds, inner, cache):
    count = zds.shape[0]
    return pl.pallas_call(
        pick_kernel,
        out_shape=jax.ShapeDtypeStruct((NY, NX, count, PAIRS, PAIR_WIDTH), jnp.bfloat16),
        grid_spec=pltpu.PrefetchScalarGridSpec(
            num_scalar_prefetch=2,
            grid=(count, NY),
            in_specs=[
                pl.BlockSpec(
                    (1, BLK_DEV, BLOCK * FEAT),
                    lambda i, y, zd, inner: (y * (NZ // 2) + zd[i] // 2, 0, 0),
                )
            ],
            out_specs=pl.BlockSpec(
                (1, NX, 1, PAIRS, PAIR_WIDTH), lambda i, y, zd, inner: (y, 0, i, 0, 0)
            ),
        ),
        compiler_params=pltpu.CompilerParams(vmem_limit_bytes=VMEM_LIMIT),
        name="pick_blocks",
    )(zds, inner, cache)


def attend_kernel(zd_ref, core_ref, blocks_ref, near_ref, far_ref, live_ref, out_ref):
    pairs = blocks_ref[:, 0].reshape(PLANE * PAIRS, PAIR_WIDTH)
    query = jnp.concatenate([near_ref[0, 0], far_ref[0, 0]], axis=0)
    shifted = pltpu.roll(query.astype(jnp.float32), KR, 1).astype(jnp.bfloat16)
    live = live_ref[0]
    width = PLANE * PAIRS
    rows = [jnp.broadcast_to(live[j : j + 1], (HEADS, width)) for j in range(RDEV)]
    valid = jnp.concatenate(rows * 2, axis=0) > 0.5
    dims = (((1,), (1,)), ((), ()))
    even_keys = pairs[:, :WIDE]
    odd_keys = pairs[:, KL:]
    even = lax.dot_general(query, even_keys, dims, preferred_element_type=jnp.float32)
    odd = lax.dot_general(shifted, odd_keys, dims, preferred_element_type=jnp.float32)
    even = jnp.where(valid, even * score_scale, EMPTY)
    odd = jnp.where(valid, odd * score_scale, EMPTY)
    top = jnp.max(jnp.maximum(even, odd), axis=1, keepdims=True)
    even = jnp.where(valid, jnp.exp(even - top), 0.0)
    odd = jnp.where(valid, jnp.exp(odd - top), 0.0)
    total = jnp.maximum(jnp.sum(even + odd, axis=1, keepdims=True), 1.0)
    value = jnp.dot(
        even.astype(jnp.bfloat16), pairs[:, :KL], preferred_element_type=jnp.float32
    )
    odd_value = jnp.dot(odd.astype(jnp.bfloat16), odd_keys, preferred_element_type=jnp.float32)
    value = (value + odd_value[:, KR : KR + KL]) * (1.0 / total)
    level = top + jnp.log(total)
    across = jnp.transpose(jnp.broadcast_to(level, (2 * ROWS_LOCAL, 128)))
    line = lax.broadcasted_iota(jnp.int32, (TAIL, ROWS_LOCAL), 0)
    for half in range(2):
        span = slice(half * ROWS_LOCAL, (half + 1) * ROWS_LOCAL)
        out_ref[0, half, :ROWS_LOCAL] = value[span].astype(jnp.bfloat16)
        wide = across[:TAIL, span]
        high = wide.astype(jnp.bfloat16).astype(jnp.float32)
        middle = (wide - high).astype(jnp.bfloat16).astype(jnp.float32)
        low = wide - high - middle
        tail = jnp.where(line == 0, high, jnp.where(line == 1, middle, jnp.where(line == 2, low, 0.0)))
        out_ref[0, half, ROWS_LOCAL:, :ROWS_LOCAL] = tail.astype(jnp.bfloat16)
        out_ref[0, half, ROWS_LOCAL:, ROWS_LOCAL:] = jnp.zeros(
            (TAIL, KL - ROWS_LOCAL), jnp.bfloat16
        )


def attend(zds, core, blocks, queries, live):
    count = zds.shape[0]
    return pl.pallas_call(
        attend_kernel,
        out_shape=jax.ShapeDtypeStruct((count, 2, ROWS_LOCAL + TAIL, KL), jnp.bfloat16),
        grid_spec=pltpu.PrefetchScalarGridSpec(
            num_scalar_prefetch=2,
            grid=(count,),
            in_specs=[
                pl.BlockSpec((PLANE, 1, PAIRS, PAIR_WIDTH), lambda i, zd, core: (0, i, 0, 0)),
                pl.BlockSpec((1, 1, ROWS_LOCAL, WIDE), lambda i, zd, core: (zd[i], core[0], 0, 0)),
                pl.BlockSpec(
                    (1, 1, ROWS_LOCAL, WIDE), lambda i, zd, core: (zd[i], 1 - core[0], 0, 0)
                ),
                pl.BlockSpec((1, RDEV, PLANE * PAIRS), lambda i, zd, core: (zd[i], 0, 0)),
            ],
            out_specs=pl.BlockSpec(
                (1, 2, ROWS_LOCAL + TAIL, KL), lambda i, zd, core: (i, 0, 0, 0)
            ),
        ),
        compiler_params=pltpu.CompilerParams(vmem_limit_bytes=VMEM_LIMIT),
        name="attend",
    )(zds, core, blocks, queries, queries, live)


def merge_kernel(*refs):
    parts, out_ref = refs[:-1], refs[-1]
    levels = []
    for part in parts:
        tail = part[ROWS_LOCAL:, :ROWS_LOCAL].astype(jnp.float32)
        levels.append(jnp.sum(tail, axis=0, keepdims=True))
    peak = functools.reduce(jnp.maximum, levels)
    weights = [jnp.exp(level - peak) for level in levels]
    scale = 1.0 / functools.reduce(jnp.add, weights)
    total = jnp.zeros((ROWS_LOCAL, KL), jnp.float32)
    for part, weight in zip(parts, weights):
        column = jnp.transpose(jnp.broadcast_to(weight * scale, (128, ROWS_LOCAL)))
        factor = jnp.concatenate([column] * (KL // 128), axis=1)
        total = total + factor * part[:ROWS_LOCAL].astype(jnp.float32)
    out_ref[...] = total.astype(jnp.bfloat16).reshape(RDEV, HEADS, KL)


def merge(parts):
    return pl.pallas_call(
        merge_kernel,
        out_shape=jax.ShapeDtypeStruct((RDEV, HEADS, KL), jnp.bfloat16),
        compiler_params=pltpu.CompilerParams(vmem_limit_bytes=VMEM_LIMIT),
        name="merge",
    )(*parts)


def per_device(queries, cache, selected):
    y, z, x = lax.axis_index("y"), lax.axis_index("z"), lax.axis_index("x")
    core = lax.axis_index("head")
    me = (y * NZ + z) * NX + x

    by_chip = selected.reshape(SEQ, RDEV * TOPK)
    inner = jnp.max(jnp.where(by_chip // BLK_DEV == me, by_chip % BLK_DEV, -1), axis=1)

    padded = jnp.pad(queries.reshape(ROWS_LOCAL, FEAT), ((0, 0), (0, KR)))
    column_queries = lax.all_gather(padded, ("z", "head"), axis=0, tiled=False)
    column_queries = column_queries.reshape(NZ, 2, ROWS_LOCAL, WIDE)

    by_place = selected.reshape(NY, NZ, NX, RDEV, TOPK) // BLK_DEV
    column_owner = lax.dynamic_index_in_dim(by_place, y, 0, keepdims=False)
    column_owner = lax.dynamic_index_in_dim(column_owner, x, 1, keepdims=False)
    slot = jnp.arange(PLANE * PAIRS, dtype=jnp.int32) // PAIRS
    holder = ((slot // NX) * NZ + z) * NX + slot % NX
    live = jnp.any(column_owner[:, :, :, None] == holder, axis=2).astype(jnp.float32)

    core_id = core.astype(jnp.int32).reshape(1)
    offsets = jnp.array(OFFSETS, jnp.int32)
    my_offsets = lax.dynamic_index_in_dim(offsets, core, 1, keepdims=False)
    targets = (z + my_offsets) % NZ

    arrived = []
    for chunk in range(len(OFFSETS)):
        picked = pick_blocks(targets[chunk], inner, cache)
        picked = picked.reshape((PLANE,) + picked.shape[2:])
        arrived.append(
            lax.all_to_all(picked, ("y", "x"), split_axis=0, concat_axis=0, tiled=True)
        )
    parts = []
    for chunk, by_core in enumerate(OFFSETS):
        partial = attend(targets[chunk], core_id, arrived[chunk], column_queries, live)
        for i in range(len(by_core[0])):
            for cross in range(2):
                route = [
                    (zz * 2 + c, ((zz + by_core[c][i]) % NZ) * 2 + (c ^ cross))
                    for zz in range(NZ)
                    for c in range(2)
                ]
                parts.append(lax.ppermute(partial[i, cross], ("z", "head"), route))
    result = merge(parts).reshape(RDEV, HEADS * KL)
    return lax.all_gather(result, "head", axis=1, tiled=True)


def solution(mesh):
    grid = Mesh(mesh.devices.reshape(NY, NZ, NX, 2), ("y", "z", "x", "head"))
    seq = ("y", "z", "x")
    placed = (P(seq, "head"), P(None, seq, None), P())
    return jax.shard_map(
        per_device, mesh=grid, in_specs=placed, out_specs=P(seq, None), check_vma=False
    )
```

```python
import functools

import jax
import jax.numpy as jnp
from jax import lax
from jax.experimental import pallas as pl
from jax.experimental.pallas import tpu as pltpu
from jax.sharding import Mesh
from jax.sharding import PartitionSpec as P

KL = 512
KR = 64
FEAT = KL + KR
WIDE = KL + 2 * KR
BLOCK = 64
PAIRS = BLOCK // 2
UNIT = PAIRS // 2
PAIR_WIDTH = 2 * FEAT
SPAN = UNIT * PAIR_WIDTH
TILES = PAIR_WIDTH // 128
TOPK = 32
RDEV = 2
BLK_DEV = 8
HEADS = 64
NY, NZ, NX = 4, 8, 4
NK = NZ // 2
GROUP = NY * 2 * NX
SEQ = NY * NZ * NX
ROWS = RDEV * HEADS
TAIL = 16
EMPTY = -1e30
MIB = 1024 * 1024

score_scale = 192.0 ** (-0.5)

STEPS = ((2, 1), (0, 3))
COUNT = len(STEPS)


def owner_of(i, meta):
    step = jnp.where(meta[2 * SEQ + 1] == 0, STEPS[i][0], STEPS[i][1])
    pair = meta[2 * SEQ] // (2 * NX) % NK
    return (pair + step) % NK * (2 * NX), meta[2 * SEQ] % (2 * NX)


def pick_kernel(i, meta_ref, cache_ref, *refs):
    out_ref = refs[-1]
    base = pl.program_id(0) * (NK * 2 * NX) + owner_of(i, meta_ref)[0]
    row = lax.broadcasted_iota(jnp.int32, (2 * NX * UNIT, BLK_DEV * UNIT), 0)
    col = lax.broadcasted_iota(jnp.int32, (2 * NX * UNIT, BLK_DEV * UNIT), 1)
    slot, token, held = row >> 4, (col >> 3) == (row & (UNIT - 1)), col & (BLK_DEV - 1)
    block = jnp.full(row.shape, -1, jnp.int32)
    for j in range(2 * NX):
        inner = jnp.maximum(meta_ref[2 * (base + j)], meta_ref[2 * (base + j) + 1])
        block = jnp.where(slot == j, inner, block)
    onehot = jnp.where(token & (held == block), 1.0, 0.0).astype(jnp.bfloat16)
    for half in range(2):
        pieces = [
            cache_ref[0, :, p * PAIR_WIDTH : (p + 1) * PAIR_WIDTH].astype(jnp.float32)
            for p in range(half * UNIT, (half + 1) * UNIT)
        ]
        stacked = jnp.concatenate(pieces, axis=0).astype(jnp.bfloat16)
        picked = jnp.dot(onehot, stacked, preferred_element_type=jnp.float32)
        picked = picked.astype(jnp.bfloat16).reshape(2 * NX, UNIT, PAIR_WIDTH)
        for t in range(TILES):
            out_ref[0, :, 0, t, half * UNIT : (half + 1) * UNIT] = picked[
                :, :, t * 128 : (t + 1) * 128
            ]


def pick_blocks(i, meta, cache, into=None, earlier=()):
    anywhere = pl.BlockSpec(memory_space=pl.ANY)
    more = () if into is None else (into,) + tuple(earlier)
    return pl.pallas_call(
        functools.partial(pick_kernel, i),
        out_shape=jax.ShapeDtypeStruct((NY, 2 * NX, COUNT, TILES, PAIRS, 128), jnp.bfloat16),
        grid_spec=pltpu.PrefetchScalarGridSpec(
            num_scalar_prefetch=1,
            grid=(NY,),
            in_specs=[
                pl.BlockSpec(
                    (1, BLK_DEV, BLOCK * FEAT),
                    lambda y, meta: (y * NK + owner_of(i, meta)[0] // (2 * NX), 0, 0),
                )
            ]
            + [anywhere] * len(more),
            out_specs=pl.BlockSpec(
                (1, 2 * NX, 1, TILES, PAIRS, 128), lambda y, meta: (y, 0, i, 0, 0, 0)
            ),
        ),
        input_output_aliases={} if into is None else {2: 0},
        compiler_params=pltpu.CompilerParams(vmem_limit_bytes=12 * MIB),
        name="pick_blocks",
    )(meta, cache, *more)


def attend_kernel(i, meta_ref, blocks_ref, near_ref, far_ref, selected_ref, _, near_out, far_out):
    width = GROUP * PAIRS
    pairs = jnp.concatenate(
        [blocks_ref[:, 0, t].reshape(width, 128) for t in range(TILES)], axis=1
    )
    query = jnp.concatenate([near_ref[...], far_ref[...]], axis=0)
    shifted = pltpu.roll(query.astype(jnp.float32), KR, 1).astype(jnp.bfloat16)
    pair, within = owner_of(i, meta_ref)
    here = meta_ref[2 * SEQ]
    owner = here // (NK * 2 * NX) * (NK * 2 * NX) + pair + within
    slot = lax.broadcasted_iota(jnp.int32, (1, width), 1) >> 5
    holder = (slot >> 3) * (NK * 2 * NX) + (here // (2 * NX) % NK * (2 * NX) + (slot & 7))
    places = selected_ref[...] >> 3
    lane = lax.broadcasted_iota(jnp.int32, places.shape, 1)
    rows = []
    for j in range(RDEV):
        mine = jnp.sum(jnp.where(lane == RDEV * owner + j, places, 0), axis=1, keepdims=True)
        read = jnp.max(jnp.where(mine == holder, 1.0, 0.0), axis=0, keepdims=True)
        rows.append(jnp.broadcast_to(read, (HEADS, width)))
    valid = jnp.concatenate(rows * 2, axis=0) > 0.5
    dims = (((1,), (1,)), ((), ()))
    odd_keys = pairs[:, KL:]
    even = lax.dot_general(query, pairs[:, :WIDE], dims, preferred_element_type=jnp.float32)
    odd = lax.dot_general(shifted, odd_keys, dims, preferred_element_type=jnp.float32)
    even = jnp.where(valid, even * score_scale, EMPTY)
    odd = jnp.where(valid, odd * score_scale, EMPTY)
    top = jnp.max(jnp.maximum(even, odd), axis=1, keepdims=True)
    even = jnp.where(valid, jnp.exp(even - top), 0.0)
    odd = jnp.where(valid, jnp.exp(odd - top), 0.0)
    total = jnp.maximum(jnp.sum(even + odd, axis=1, keepdims=True), 1.0)
    value = jnp.dot(
        even.astype(jnp.bfloat16), pairs[:, :KL], preferred_element_type=jnp.float32
    )
    odd_value = jnp.dot(odd.astype(jnp.bfloat16), odd_keys, preferred_element_type=jnp.float32)
    value = (value + odd_value[:, KR : KR + KL]) * (1.0 / total)
    value = value.astype(jnp.bfloat16)
    level = top + jnp.log(total)
    across = jnp.transpose(jnp.broadcast_to(level, (2 * ROWS, 128)))[:TAIL]
    for half, out_ref in enumerate((near_out, far_out)):
        span = slice(half * ROWS, (half + 1) * ROWS)
        wide = across[:, span]
        high = wide.astype(jnp.bfloat16).astype(jnp.float32)
        middle = (wide - high).astype(jnp.bfloat16).astype(jnp.float32)
        low = wide - high - middle
        line = lax.broadcasted_iota(jnp.int32, wide.shape, 0)
        tail = jnp.where(
            line == 0, high, jnp.where(line == 1, middle, jnp.where(line == 2, low, 0.0))
        )
        out_ref[:ROWS] = value[span]
        out_ref[ROWS:, :ROWS] = tail.astype(jnp.bfloat16)
        out_ref[ROWS:, ROWS:] = jnp.zeros((TAIL, KL - ROWS), jnp.bfloat16)


def attend(i, meta, blocks, near, far, selected, earlier):
    part = jax.ShapeDtypeStruct((ROWS + TAIL, KL), jnp.bfloat16)
    query = pl.BlockSpec((ROWS, WIDE), lambda n, meta: (0, 0))
    return pl.pallas_call(
        functools.partial(attend_kernel, i),
        out_shape=[part, part],
        grid_spec=pltpu.PrefetchScalarGridSpec(
            num_scalar_prefetch=1,
            grid=(1,),
            in_specs=[
                pl.BlockSpec((GROUP, 1, TILES, PAIRS, 128), lambda n, meta: (0, i, 0, 0, 0)),
                query,
                query,
                pl.BlockSpec(selected.shape, lambda n, meta: (0, 0)),
                pl.BlockSpec(memory_space=pl.ANY),
            ],
            out_specs=[pl.BlockSpec((ROWS + TAIL, KL), lambda n, meta: (0, 0))] * 2,
        ),
        compiler_params=pltpu.CompilerParams(vmem_limit_bytes=24 * MIB),
        cost_estimate=pl.CostEstimate(flops=1, bytes_accessed=1, transcendentals=0),
        name="attend",
    )(meta, blocks, near, far, selected, earlier)


def weigh(parts, levels):
    peak = functools.reduce(jnp.maximum, levels)
    weights = [jnp.exp(level - peak) for level in levels]
    total = functools.reduce(jnp.add, weights)
    scale = 1.0 / total
    mean = jnp.zeros((ROWS, KL), jnp.float32)
    for part, weight in zip(parts, weights):
        column = jnp.transpose(jnp.broadcast_to(weight * scale, (128, ROWS)))
        factor = jnp.concatenate([column] * (KL // 128), axis=1)
        mean = mean + factor * part[:ROWS].astype(jnp.float32)
    return mean, peak + jnp.log(total)


def level_of(part):
    return jnp.sum(part[ROWS:, :ROWS].astype(jnp.float32), axis=0, keepdims=True)


def premerge_kernel(*refs):
    parts, out_ref = refs[:-1], refs[-1]
    mean, level = weigh(parts, [level_of(part) for part in parts])
    out_ref[:ROWS] = mean
    out_ref[ROWS:, :ROWS] = jnp.broadcast_to(level, (8, ROWS))
    out_ref[ROWS:, ROWS:] = jnp.zeros((8, KL - ROWS), jnp.float32)


def premerge(parts):
    return pl.pallas_call(
        premerge_kernel,
        out_shape=jax.ShapeDtypeStruct((ROWS + 8, KL), jnp.float32),
        compiler_params=pltpu.CompilerParams(vmem_limit_bytes=8 * MIB),
        name="premerge",
    )(*parts)


def merge_kernel(state, *refs):
    parts, out_ref = refs[:-1], refs[-1]
    levels = [state[ROWS : ROWS + 1, :ROWS]] + [level_of(part) for part in parts]
    mean, _ = weigh((state,) + parts, levels)
    out_ref[...] = mean.astype(jnp.bfloat16).reshape(RDEV, HEADS, KL)


def merge(parts):
    return pl.pallas_call(
        merge_kernel,
        out_shape=jax.ShapeDtypeStruct((RDEV, HEADS, KL), jnp.bfloat16),
        compiler_params=pltpu.CompilerParams(vmem_limit_bytes=8 * MIB),
        name="merge",
    )(*parts)


def per_device(queries, cache, selected):
    y, zhi, zlo, x = (lax.axis_index(name) for name in ("y", "zhi", "zlo", "x"))
    core = lax.axis_index("head")
    me = ((y * NK + zhi) * 2 + zlo) * NX + x

    extended = jnp.pad(selected, ((0, 8), (0, 0)), constant_values=-1)
    which = lax.broadcasted_iota(jnp.int32, extended.shape, 0)
    local = jnp.where(extended // BLK_DEV == me, extended % BLK_DEV, -1)
    local = jnp.where(which == 2 * SEQ, me, jnp.where(which == 2 * SEQ + 1, core, local))
    meta = jnp.max(local, axis=1)

    def route(steps, back, cross):
        pairs = [
            (zz * 2 + c, (zz + steps[c]) % NK * 2 + (c ^ cross)) for zz in range(NK) for c in range(2)
        ]
        return [pair[::-1] for pair in pairs] if back else pairs

    def move(value, *way):
        return lax.ppermute(value, ("zhi", "head"), route(*way))

    padded = jnp.pad(queries.reshape(ROWS, FEAT), ((0, 0), (0, KR)))
    asked = [move(padded, steps, True, cross) for steps in STEPS for cross in range(2)]
    picked = pick_blocks(0, meta, cache)
    picked = pick_blocks(1, meta, cache, picked, asked)
    picked = picked.reshape(GROUP, COUNT * TILES * PAIRS, 128)
    blocks = lax.all_to_all(picked, ("y", "zlo", "x"), split_axis=0, concat_axis=0, tiled=True)
    blocks = blocks.reshape(GROUP, COUNT, TILES, PAIRS, 128)

    parts, earlier = [], meta
    for i, steps in enumerate(STEPS):
        near, far = attend(i, meta, blocks, asked[2 * i], asked[2 * i + 1], selected.T, earlier)
        parts.append([move(near, steps, False, 0), move(far, steps, False, 1)])
        earlier = near
    result = merge([premerge(parts[0])] + parts[1]).reshape(RDEV, HEADS * KL)
    return lax.all_gather(result, "head", axis=1, tiled=True)


def solution(mesh):
    grid = Mesh(mesh.devices.reshape(NY, NK, 2, NX, 2), ("y", "zhi", "zlo", "x", "head"))
    seq = ("y", "zhi", "zlo", "x")
    placed = (P(seq, "head"), P(None, seq, None), P())
    return jax.shard_map(
        per_device, mesh=grid, in_specs=placed, out_specs=P(seq, None), check_vma=False
    )
```

```python
import functools

import jax
import jax.numpy as jnp
from jax import lax
from jax.experimental import pallas as pl
from jax.experimental.pallas import tpu as pltpu
from jax.sharding import Mesh
from jax.sharding import PartitionSpec as P

KL = 512
KR = 64
FEAT = KL + KR
WIDE = KL + 2 * KR
BLOCK = 64
PAIRS = BLOCK // 2
UNIT = PAIRS // 2
PAIR_WIDTH = 2 * FEAT
SPAN = UNIT * PAIR_WIDTH
TILES = PAIR_WIDTH // 128
TOPK = 32
RDEV = 2
BLK_DEV = 8
HEADS = 64
NY, NZ, NX = 4, 8, 4
NK = NZ // 2
GROUP = NY * 2 * NX
SEQ = NY * NZ * NX
ROWS = RDEV * HEADS
TAIL = 16
EMPTY = -1e30
MIB = 1024 * 1024

score_scale = 192.0 ** (-0.5)

COUNT = 2


def owner_place(zhi, zlo, core, i):
    if core == 0:
        return ((zhi + 2) % NK, 1 - zlo) if i == 0 else (zhi, zlo)
    return (zhi + 3 - 2 * zlo) % NK, zlo if i == 0 else 1 - zlo


def own_place(meta):
    here = meta[2 * SEQ]
    return here // (2 * NX) % NK, here // NX % 2, meta[2 * SEQ + 1]


def pick_pair(n, meta):
    zhi, _, core = own_place(meta)
    return (zhi + jnp.where(core == 0, 2 - 2 * n, 3 - 2 * n)) % NK


def pick_kernel(meta_ref, cache_ref, out_ref):
    n = pl.program_id(1)
    core = meta_ref[2 * SEQ + 1]
    base = (pl.program_id(0) * NK + pick_pair(n, meta_ref)) * (2 * NX)
    row = lax.broadcasted_iota(jnp.int32, (2 * NX * UNIT, BLK_DEV * UNIT), 0)
    col = lax.broadcasted_iota(jnp.int32, (2 * NX * UNIT, BLK_DEV * UNIT), 1)
    slot, token, held = row >> 4, (col >> 3) == (row & (UNIT - 1)), col & (BLK_DEV - 1)
    block = jnp.full(row.shape, -1, jnp.int32)
    for j in range(2 * NX):
        inner = jnp.maximum(meta_ref[2 * (base + j)], meta_ref[2 * (base + j) + 1])
        block = jnp.where(slot == j, inner, block)
    onehot = jnp.where(token & (held == block), 1.0, 0.0).astype(jnp.bfloat16)
    for half in range(2):
        pieces = [
            cache_ref[0, :, p * PAIR_WIDTH : (p + 1) * PAIR_WIDTH].astype(jnp.float32)
            for p in range(half * UNIT, (half + 1) * UNIT)
        ]
        stacked = jnp.concatenate(pieces, axis=0).astype(jnp.bfloat16)
        picked = jnp.dot(onehot, stacked, preferred_element_type=jnp.float32)
        picked = picked.astype(jnp.bfloat16).reshape(2, NX, UNIT, PAIR_WIDTH)
        for zlo in range(2):
            chip = jnp.where(core == 0, jnp.where(n == 0, 1 - zlo, zlo), n)
            index = jnp.where(core == 0, n, jnp.where(n == zlo, 0, 1))
            for t in range(TILES):
                out_ref[0, pl.ds(chip * NX, NX), index, t, half * UNIT : (half + 1) * UNIT] = picked[
                    zlo, :, :, t * 128 : (t + 1) * 128
                ]


def pick_blocks(meta, cache):
    return pl.pallas_call(
        pick_kernel,
        out_shape=jax.ShapeDtypeStruct((NY, 2 * NX, COUNT, TILES, PAIRS, 128), jnp.bfloat16),
        grid_spec=pltpu.PrefetchScalarGridSpec(
            num_scalar_prefetch=1,
            grid=(NY, COUNT),
            in_specs=[
                pl.BlockSpec(
                    (1, BLK_DEV, BLOCK * FEAT),
                    lambda y, n, meta: (y * NK + pick_pair(n, meta), 0, 0),
                )
            ],
            out_specs=pl.BlockSpec(
                (1, 2 * NX, COUNT, TILES, PAIRS, 128), lambda y, n, meta: (y, 0, 0, 0, 0, 0)
            ),
        ),
        compiler_params=pltpu.CompilerParams(vmem_limit_bytes=12 * MIB),
        name="pick_blocks",
    )(meta, cache)


def tie_kernel(*refs):
    pass


def tie(value, *earlier):
    anywhere = pl.BlockSpec(memory_space=pl.ANY)
    return pl.pallas_call(
        tie_kernel,
        out_shape=jax.ShapeDtypeStruct(value.shape, value.dtype),
        in_specs=[anywhere] * (1 + len(earlier)),
        out_specs=anywhere,
        input_output_aliases={0: 0},
        compiler_params=pltpu.CompilerParams(vmem_limit_bytes=MIB),
        name="tie",
    )(value, *earlier)


def spread_queries(packed):
    lane = lax.broadcasted_iota(jnp.int32, (RDEV * HEADS // 2, WIDE), 1)
    even = jnp.where(lane < FEAT, packed[:, :WIDE].astype(jnp.float32), 0.0)
    odd = jnp.where(lane >= KR, packed[:, KL:].astype(jnp.float32), 0.0)
    low = [even, pltpu.roll(odd, FEAT, 1)]
    high = [pltpu.roll(even, KR, 1), odd]
    return low, high


def attend_kernel(i, meta_ref, blocks_ref, near_ref, far_ref, selected_ref, _, near_out, far_out):
    width = GROUP * PAIRS
    pairs = jnp.concatenate(
        [blocks_ref[:, 0, t].reshape(width, 128) for t in range(TILES)], axis=1
    )
    low, high = [], []
    for ref in (near_ref, far_ref):
        parts = spread_queries(ref[...])
        low += parts[0]
        high += parts[1]
    query = jnp.concatenate(low, axis=0).astype(jnp.bfloat16)
    shifted = jnp.concatenate(high, axis=0).astype(jnp.bfloat16)
    zhi, zlo, core = own_place(meta_ref)
    here = meta_ref[2 * SEQ]
    first, second = (owner_place(zhi, zlo, c, i) for c in range(2))
    pair = jnp.where(core == 0, first[0], second[0])
    chip = jnp.where(core == 0, first[1], second[1])
    owner = here // (NK * 2 * NX) * (NK * 2 * NX) + pair * (2 * NX) + chip * NX + here % NX
    slot = lax.broadcasted_iota(jnp.int32, (1, width), 1) >> 5
    holder = (slot >> 3) * (NK * 2 * NX) + (zhi * (2 * NX) + (slot & 7))
    places = selected_ref[...] >> 3
    lane = lax.broadcasted_iota(jnp.int32, places.shape, 1)
    rows = []
    for j in range(RDEV):
        mine = jnp.sum(jnp.where(lane == RDEV * owner + j, places, 0), axis=1, keepdims=True)
        read = jnp.max(jnp.where(mine == holder, 1.0, 0.0), axis=0, keepdims=True)
        rows.append(jnp.broadcast_to(read, (HEADS // 2, width)))
    valid = jnp.concatenate(rows * 4, axis=0) > 0.5
    dims = (((1,), (1,)), ((), ()))
    odd_keys = pairs[:, KL:]
    even = lax.dot_general(query, pairs[:, :WIDE], dims, preferred_element_type=jnp.float32)
    odd = lax.dot_general(shifted, odd_keys, dims, preferred_element_type=jnp.float32)
    even = jnp.where(valid, even * score_scale, EMPTY)
    odd = jnp.where(valid, odd * score_scale, EMPTY)
    top = jnp.max(jnp.maximum(even, odd), axis=1, keepdims=True)
    even = jnp.where(valid, jnp.exp(even - top), 0.0)
    odd = jnp.where(valid, jnp.exp(odd - top), 0.0)
    total = jnp.maximum(jnp.sum(even + odd, axis=1, keepdims=True), 1.0)
    value = jnp.dot(
        even.astype(jnp.bfloat16), pairs[:, :KL], preferred_element_type=jnp.float32
    )
    odd_value = jnp.dot(odd.astype(jnp.bfloat16), odd_keys, preferred_element_type=jnp.float32)
    value = (value + odd_value[:, KR : KR + KL]) * (1.0 / total)
    value = value.astype(jnp.bfloat16)
    level = top + jnp.log(total)
    across = jnp.transpose(jnp.broadcast_to(level, (2 * ROWS, 128)))[:TAIL]
    for half, out_ref in enumerate((near_out, far_out)):
        span = slice(half * ROWS, (half + 1) * ROWS)
        wide = across[:, span]
        high = wide.astype(jnp.bfloat16).astype(jnp.float32)
        middle = (wide - high).astype(jnp.bfloat16).astype(jnp.float32)
        low = wide - high - middle
        line = lax.broadcasted_iota(jnp.int32, wide.shape, 0)
        tail = jnp.where(
            line == 0, high, jnp.where(line == 1, middle, jnp.where(line == 2, low, 0.0))
        )
        out_ref[:ROWS] = value[span]
        out_ref[ROWS:, :ROWS] = tail.astype(jnp.bfloat16)
        out_ref[ROWS:, ROWS:] = jnp.zeros((TAIL, KL - ROWS), jnp.bfloat16)


def attend(i, meta, blocks, near, far, selected, earlier):
    part = jax.ShapeDtypeStruct((ROWS + TAIL, KL), jnp.bfloat16)
    query = pl.BlockSpec((ROWS // 2, PAIR_WIDTH), lambda n, meta: (0, 0))
    return pl.pallas_call(
        functools.partial(attend_kernel, i),
        out_shape=[part, part],
        grid_spec=pltpu.PrefetchScalarGridSpec(
            num_scalar_prefetch=1,
            grid=(1,),
            in_specs=[
                pl.BlockSpec((GROUP, 1, TILES, PAIRS, 128), lambda n, meta: (0, i, 0, 0, 0)),
                query,
                query,
                pl.BlockSpec(selected.shape, lambda n, meta: (0, 0)),
                pl.BlockSpec(memory_space=pl.ANY),
            ],
            out_specs=[pl.BlockSpec((ROWS + TAIL, KL), lambda n, meta: (0, 0))] * 2,
        ),
        compiler_params=pltpu.CompilerParams(vmem_limit_bytes=24 * MIB),
        cost_estimate=pl.CostEstimate(flops=1, bytes_accessed=1, transcendentals=0),
        name="attend",
    )(meta, blocks, near, far, selected, earlier)


def weigh(parts, levels):
    peak = functools.reduce(jnp.maximum, levels)
    weights = [jnp.exp(level - peak) for level in levels]
    total = functools.reduce(jnp.add, weights)
    scale = 1.0 / total
    mean = jnp.zeros((ROWS, KL), jnp.float32)
    for part, weight in zip(parts, weights):
        column = jnp.transpose(jnp.broadcast_to(weight * scale, (128, ROWS)))
        factor = jnp.concatenate([column] * (KL // 128), axis=1)
        mean = mean + factor * part[:ROWS].astype(jnp.float32)
    return mean, peak + jnp.log(total)


def level_of(part):
    return jnp.sum(part[ROWS:, :ROWS].astype(jnp.float32), axis=0, keepdims=True)


def premerge_kernel(*refs):
    parts, out_ref = refs[:-1], refs[-1]
    mean, level = weigh(parts, [level_of(part) for part in parts])
    out_ref[:ROWS] = mean
    out_ref[ROWS:, :ROWS] = jnp.broadcast_to(level, (8, ROWS))
    out_ref[ROWS:, ROWS:] = jnp.zeros((8, KL - ROWS), jnp.float32)


def premerge(parts):
    return pl.pallas_call(
        premerge_kernel,
        out_shape=jax.ShapeDtypeStruct((ROWS + 8, KL), jnp.float32),
        compiler_params=pltpu.CompilerParams(vmem_limit_bytes=8 * MIB),
        name="premerge",
    )(*parts)


def merge_kernel(state, *refs):
    parts, out_ref = refs[:-1], refs[-1]
    levels = [state[ROWS : ROWS + 1, :ROWS]] + [level_of(part) for part in parts]
    mean, _ = weigh((state,) + parts, levels)
    mean = mean.astype(jnp.bfloat16).reshape(2, RDEV, HEADS // 2, KL)
    for odd in range(2):
        out_ref[:, :, odd * KL : (odd + 1) * KL] = mean[odd]


def merge(parts):
    return pl.pallas_call(
        merge_kernel,
        out_shape=jax.ShapeDtypeStruct((RDEV, HEADS // 2, 2 * KL), jnp.bfloat16),
        compiler_params=pltpu.CompilerParams(vmem_limit_bytes=8 * MIB),
        name="merge",
    )(*parts)


def per_device(queries, cache, selected):
    y, zhi, zlo, x = (lax.axis_index(name) for name in ("y", "zhi", "zlo", "x"))
    core = lax.axis_index("head")
    me = ((y * NK + zhi) * 2 + zlo) * NX + x

    extended = jnp.pad(selected, ((0, 8), (0, 0)), constant_values=-1)
    which = lax.broadcasted_iota(jnp.int32, extended.shape, 0)
    local = jnp.where(extended // BLK_DEV == me, extended % BLK_DEV, -1)
    local = jnp.where(which == 2 * SEQ, me, jnp.where(which == 2 * SEQ + 1, core, local))
    meta = jnp.max(local, axis=1)

    def move(value, i, back, cross):
        pairs = []
        for zz in range(NZ):
            for c in range(2):
                pair, chip = owner_place(zz // 2, zz % 2, c, i)
                pairs.append((zz * 2 + c, (pair * 2 + chip) * 2 + (c ^ cross)))
        pairs = [pair[::-1] for pair in pairs] if back else pairs
        return lax.ppermute(value, ("zhi", "zlo", "head"), pairs)

    packed = queries.reshape(ROWS // 2, PAIR_WIDTH)
    asked = {}
    for i in (1, 0):
        for cross in (1, 0):
            asked[i, cross] = move(packed, i, True, cross)
    picked = tie(pick_blocks(meta, cache), *asked.values())
    picked = picked.reshape(GROUP, COUNT * TILES * PAIRS, 128)
    blocks = lax.all_to_all(picked, ("y", "zlo", "x"), split_axis=0, concat_axis=0, tiled=True)
    blocks = blocks.reshape(GROUP, COUNT, TILES, PAIRS, 128)

    parts, earlier = [], meta
    for i in range(COUNT):
        near, far = attend(i, meta, blocks, asked[i, 0], asked[i, 1], selected.T, earlier)
        parts.append([move(near, i, False, 0), move(far, i, False, 1)])
        earlier = near
    result = merge([premerge(parts[0])] + parts[1]).reshape(RDEV, HEADS * KL)
    return lax.all_gather(result, "head", axis=1, tiled=True)


def solution(mesh):
    grid = Mesh(mesh.devices.reshape(NY, NK, 2, NX, 2), ("y", "zhi", "zlo", "x", "head"))
    seq = ("y", "zhi", "zlo", "x")
    placed = (P(seq, "head"), P(None, seq, None), P())
    return jax.shard_map(
        per_device, mesh=grid, in_specs=placed, out_specs=P(seq, None), check_vma=False
    )
```

```python
import functools

import jax
import jax.numpy as jnp
from jax import lax
from jax.experimental import pallas as pl
from jax.experimental.pallas import tpu as pltpu
from jax.sharding import Mesh
from jax.sharding import PartitionSpec as P

KL = 512
KR = 64
FEAT = KL + KR
WIDE = KL + 2 * KR
BLOCK = 64
PAIRS = BLOCK // 2
UNIT = PAIRS // 2
PAIR_WIDTH = 2 * FEAT
SPAN = UNIT * PAIR_WIDTH
TILES = PAIR_WIDTH // 128
TOPK = 32
RDEV = 2
BLK_DEV = 8
HEADS = 64
NY, NZ, NX = 4, 8, 4
NK = NZ // 2
GROUP = NY * 2 * NX
SEQ = NY * NZ * NX
ROWS = RDEV * HEADS
TAIL = 16
EMPTY = -1e30
MIB = 1024 * 1024

score_scale = 192.0 ** (-0.5)

COUNT = 2


def owner_place(zhi, zlo, core, i):
    if core == 0:
        return ((zhi + 2) % NK, 1 - zlo) if i == 0 else (zhi, zlo)
    return (zhi + 3 - 2 * zlo) % NK, zlo if i == 0 else 1 - zlo


def own_place(meta):
    here = meta[2 * SEQ]
    return here // (2 * NX) % NK, here // NX % 2, meta[2 * SEQ + 1]


def pick_pair(n, meta):
    zhi, _, core = own_place(meta)
    return (zhi + jnp.where(core == 0, 2 - 2 * n, 3 - 2 * n)) % NK


def pick_kernel(meta_ref, cache_ref, out_ref, held_ref, sems):
    y, n = pl.program_id(0), pl.program_id(1)

    def fetch(y, n):
        place = y * COUNT + n
        request = y * NK + pick_pair(n, meta_ref)
        return pltpu.make_async_copy(cache_ref.at[request], held_ref.at[place], sems.at[place])

    @pl.when((y == 0) & (n == 0))
    def _():
        for yy in range(NY):
            for nn in range(COUNT):
                fetch(yy, nn).start(priority=nn)

    core = meta_ref[2 * SEQ + 1]
    base = (y * NK + pick_pair(n, meta_ref)) * (2 * NX)
    row = lax.broadcasted_iota(jnp.int32, (2 * NX * UNIT, BLK_DEV * UNIT), 0)
    col = lax.broadcasted_iota(jnp.int32, (2 * NX * UNIT, BLK_DEV * UNIT), 1)
    slot, token, held = row >> 4, (col >> 3) == (row & (UNIT - 1)), col & (BLK_DEV - 1)
    block = jnp.full(row.shape, -1, jnp.int32)
    for j in range(2 * NX):
        inner = jnp.maximum(meta_ref[2 * (base + j)], meta_ref[2 * (base + j) + 1])
        block = jnp.where(slot == j, inner, block)
    onehot = jnp.where(token & (held == block), 1.0, 0.0).astype(jnp.bfloat16)
    fetch(y, n).wait()
    for half in range(2):
        pieces = [
            held_ref[y * COUNT + n, :, p * PAIR_WIDTH : (p + 1) * PAIR_WIDTH].astype(jnp.float32)
            for p in range(half * UNIT, (half + 1) * UNIT)
        ]
        stacked = jnp.concatenate(pieces, axis=0).astype(jnp.bfloat16)
        picked = jnp.dot(onehot, stacked, preferred_element_type=jnp.float32)
        picked = picked.astype(jnp.bfloat16).reshape(2, NX, UNIT, PAIR_WIDTH)
        for zlo in range(2):
            chip = jnp.where(core == 0, jnp.where(n == 0, 1 - zlo, zlo), n)
            index = jnp.where(core == 0, n, jnp.where(n == zlo, 0, 1))
            for t in range(TILES):
                out_ref[0, pl.ds(chip * NX, NX), index, t, half * UNIT : (half + 1) * UNIT] = picked[
                    zlo, :, :, t * 128 : (t + 1) * 128
                ]


def pick_blocks(meta, cache):
    return pl.pallas_call(
        pick_kernel,
        out_shape=jax.ShapeDtypeStruct((NY, 2 * NX, COUNT, TILES, PAIRS, 128), jnp.bfloat16),
        grid_spec=pltpu.PrefetchScalarGridSpec(
            num_scalar_prefetch=1,
            grid=(NY, COUNT),
            in_specs=[pl.BlockSpec(memory_space=pl.ANY)],
            out_specs=pl.BlockSpec(
                (1, 2 * NX, COUNT, TILES, PAIRS, 128), lambda y, n, meta: (y, 0, 0, 0, 0, 0)
            ),
            scratch_shapes=[
                pltpu.VMEM((NY * COUNT, BLK_DEV, BLOCK * FEAT), jnp.bfloat16),
                pltpu.SemaphoreType.DMA((NY * COUNT,)),
            ],
        ),
        compiler_params=pltpu.CompilerParams(vmem_limit_bytes=46 * MIB),
        name="pick_blocks",
    )(meta, cache)


def tie_kernel(*refs):
    pass


def tie(value, *earlier):
    anywhere = pl.BlockSpec(memory_space=pl.ANY)
    return pl.pallas_call(
        tie_kernel,
        out_shape=jax.ShapeDtypeStruct(value.shape, value.dtype),
        in_specs=[anywhere] * (1 + len(earlier)),
        out_specs=anywhere,
        input_output_aliases={0: 0},
        compiler_params=pltpu.CompilerParams(vmem_limit_bytes=MIB),
        name="tie",
    )(value, *earlier)


def spread_queries(packed):
    lane = lax.broadcasted_iota(jnp.int32, (RDEV * HEADS // 2, WIDE), 1)
    even = jnp.where(lane < FEAT, packed[:, :WIDE].astype(jnp.float32), 0.0)
    odd = jnp.where(lane >= KR, packed[:, KL:].astype(jnp.float32), 0.0)
    low = [even, pltpu.roll(odd, FEAT, 1)]
    high = [pltpu.roll(even, KR, 1), odd]
    return low, high


def attend_kernel(i, meta_ref, blocks_ref, queries_ref, selected_ref, _, out_ref):
    width = GROUP * PAIRS
    pairs = jnp.concatenate(
        [blocks_ref[:, 0, t].reshape(width, 128) for t in range(TILES)], axis=1
    )
    low, high = [], []
    for half in range(2):
        parts = spread_queries(queries_ref[half])
        low += parts[0]
        high += parts[1]
    query = jnp.concatenate(low, axis=0).astype(jnp.bfloat16)
    shifted = jnp.concatenate(high, axis=0).astype(jnp.bfloat16)
    zhi, zlo, core = own_place(meta_ref)
    here = meta_ref[2 * SEQ]
    first, second = (owner_place(zhi, zlo, c, i) for c in range(2))
    pair = jnp.where(core == 0, first[0], second[0])
    chip = jnp.where(core == 0, first[1], second[1])
    owner = here // (NK * 2 * NX) * (NK * 2 * NX) + pair * (2 * NX) + chip * NX + here % NX
    slot = lax.broadcasted_iota(jnp.int32, (1, width), 1) >> 5
    holder = (slot >> 3) * (NK * 2 * NX) + (zhi * (2 * NX) + (slot & 7))
    places = selected_ref[...] >> 3
    lane = lax.broadcasted_iota(jnp.int32, places.shape, 1)
    rows = []
    for j in range(RDEV):
        mine = jnp.sum(jnp.where(lane == RDEV * owner + j, places, 0), axis=1, keepdims=True)
        read = jnp.max(jnp.where(mine == holder, 1.0, 0.0), axis=0, keepdims=True)
        rows.append(jnp.broadcast_to(read, (HEADS // 2, width)))
    valid = jnp.concatenate(rows * 4, axis=0) > 0.5
    dims = (((1,), (1,)), ((), ()))
    odd_keys = pairs[:, KL:]
    even = lax.dot_general(query, pairs[:, :WIDE], dims, preferred_element_type=jnp.float32)
    odd = lax.dot_general(shifted, odd_keys, dims, preferred_element_type=jnp.float32)
    even = jnp.where(valid, even * score_scale, EMPTY)
    odd = jnp.where(valid, odd * score_scale, EMPTY)
    top = jnp.max(jnp.maximum(even, odd), axis=1, keepdims=True)
    even = jnp.where(valid, jnp.exp(even - top), 0.0)
    odd = jnp.where(valid, jnp.exp(odd - top), 0.0)
    total = jnp.maximum(jnp.sum(even + odd, axis=1, keepdims=True), 1.0)
    value = jnp.dot(
        even.astype(jnp.bfloat16), pairs[:, :KL], preferred_element_type=jnp.float32
    )
    odd_value = jnp.dot(odd.astype(jnp.bfloat16), odd_keys, preferred_element_type=jnp.float32)
    value = (value + odd_value[:, KR : KR + KL]) * (1.0 / total)
    level = top + jnp.log(total)
    wide = jnp.transpose(jnp.broadcast_to(level, (2 * ROWS, 128)))[:TAIL]
    high = wide.astype(jnp.bfloat16).astype(jnp.float32)
    middle = (wide - high).astype(jnp.bfloat16).astype(jnp.float32)
    low = wide - high - middle
    line = lax.broadcasted_iota(jnp.int32, wide.shape, 0)
    tail = jnp.where(line == 0, high, jnp.where(line == 1, middle, jnp.where(line == 2, low, 0.0)))
    out_ref[: 2 * ROWS] = value.astype(jnp.bfloat16)
    out_ref[2 * ROWS :, : 2 * ROWS] = tail.astype(jnp.bfloat16)
    out_ref[2 * ROWS :, 2 * ROWS :] = jnp.zeros((TAIL, KL - 2 * ROWS), jnp.bfloat16)


def attend(i, meta, blocks, queries, selected, earlier):
    shape = (2 * ROWS + TAIL, KL)
    return pl.pallas_call(
        functools.partial(attend_kernel, i),
        out_shape=jax.ShapeDtypeStruct(shape, jnp.bfloat16),
        grid_spec=pltpu.PrefetchScalarGridSpec(
            num_scalar_prefetch=1,
            grid=(1,),
            in_specs=[
                pl.BlockSpec((GROUP, 1, TILES, PAIRS, 128), lambda n, meta: (0, i, 0, 0, 0)),
                pl.BlockSpec(queries.shape, lambda n, meta: (0, 0, 0)),
                pl.BlockSpec(selected.shape, lambda n, meta: (0, 0)),
                pl.BlockSpec(memory_space=pl.ANY),
            ],
            out_specs=pl.BlockSpec(shape, lambda n, meta: (0, 0)),
        ),
        compiler_params=pltpu.CompilerParams(vmem_limit_bytes=24 * MIB),
        cost_estimate=pl.CostEstimate(flops=1, bytes_accessed=1, transcendentals=0),
        name="attend",
    )(meta, blocks, queries, selected, earlier)


def weigh(values, levels):
    peak = functools.reduce(jnp.maximum, levels)
    weights = [jnp.exp(level - peak) for level in levels]
    total = functools.reduce(jnp.add, weights)
    scale = 1.0 / total
    mean = jnp.zeros((ROWS, KL), jnp.float32)
    for value, weight in zip(values, weights):
        column = jnp.transpose(jnp.broadcast_to(weight * scale, (128, ROWS)))
        factor = jnp.concatenate([column] * (KL // 128), axis=1)
        mean = mean + factor * value.astype(jnp.float32)
    return mean, peak + jnp.log(total)


def halves_of(ref, half):
    tail = ref[2 * ROWS :, half * ROWS : (half + 1) * ROWS].astype(jnp.float32)
    return ref[half * ROWS : (half + 1) * ROWS], jnp.sum(tail, axis=0, keepdims=True)


def premerge_kernel(mine_ref, other_ref, out_ref):
    for half in range(2):
        views = [halves_of(mine_ref, half), halves_of(other_ref, 1 - half)]
        mean, level = weigh([view[0] for view in views], [view[1] for view in views])
        out_ref[half, :ROWS] = mean
        out_ref[half, ROWS:, :ROWS] = jnp.broadcast_to(level, (8, ROWS))
        out_ref[half, ROWS:, ROWS:] = jnp.zeros((8, KL - ROWS), jnp.float32)


def premerge(mine, other):
    return pl.pallas_call(
        premerge_kernel,
        out_shape=jax.ShapeDtypeStruct((2, ROWS + 8, KL), jnp.float32),
        compiler_params=pltpu.CompilerParams(vmem_limit_bytes=8 * MIB),
        name="premerge",
    )(mine, other)


def merge_kernel(meta_ref, state_ref, mine_ref, other_ref, out_ref):
    core = meta_ref[2 * SEQ + 1]
    for half in range(2):
        state = (state_ref[half, :ROWS], state_ref[half, ROWS : ROWS + 1, :ROWS])
        views = [state, halves_of(mine_ref, half), halves_of(other_ref, 1 - half)]
        mean, _ = weigh([view[0] for view in views], [view[1] for view in views])
        mean = mean.astype(jnp.bfloat16).reshape(2, RDEV, HEADS // 2, KL)
        for odd in range(2):
            out_ref[:, core ^ half, :, odd * KL : (odd + 1) * KL] = mean[odd]


def merge(meta, parts):
    shape = (RDEV, 2, HEADS // 2, 2 * KL)
    return pl.pallas_call(
        merge_kernel,
        out_shape=jax.ShapeDtypeStruct(shape, jnp.bfloat16),
        grid_spec=pltpu.PrefetchScalarGridSpec(
            num_scalar_prefetch=1,
            grid=(1,),
            in_specs=[
                pl.BlockSpec(part.shape, lambda n, meta, rank=part.ndim: (0,) * rank)
                for part in parts
            ],
            out_specs=pl.BlockSpec(shape, lambda n, meta: (0, 0, 0, 0)),
        ),
        compiler_params=pltpu.CompilerParams(vmem_limit_bytes=12 * MIB),
        name="merge",
    )(meta, *parts)


def per_device(queries, cache, selected):
    y, zhi, zlo, x = (lax.axis_index(name) for name in ("y", "zhi", "zlo", "x"))
    core = lax.axis_index("head")
    me = ((y * NK + zhi) * 2 + zlo) * NX + x

    extended = jnp.pad(selected, ((0, 8), (0, 0)), constant_values=-1)
    which = lax.broadcasted_iota(jnp.int32, extended.shape, 0)
    local = jnp.where(extended // BLK_DEV == me, extended % BLK_DEV, -1)
    local = jnp.where(which == 2 * SEQ, me, jnp.where(which == 2 * SEQ + 1, core, local))
    meta = jnp.max(local, axis=1)

    def move(value, i, back, cross):
        pairs = []
        for zz in range(NZ):
            for c in range(2):
                pair, chip = owner_place(zz // 2, zz % 2, c, i)
                pairs.append((zz * 2 + c, (pair * 2 + chip) * 2 + (c ^ cross)))
        pairs = [pair[::-1] for pair in pairs] if back else pairs
        return lax.ppermute(value, ("zhi", "zlo", "head"), pairs)

    swap = [(0, 1), (1, 0)]
    packed = queries.reshape(ROWS // 2, PAIR_WIDTH)
    both = jnp.stack([packed, lax.ppermute(packed, "head", swap)])
    asked = [jnp.stack([move(packed, 0, True, cross) for cross in range(2)])]
    picked = tie(pick_blocks(meta, cache), *asked, both)
    picked = picked.reshape(GROUP, COUNT * TILES * PAIRS, 128)
    blocks = lax.all_to_all(picked, ("y", "zlo", "x"), split_axis=0, concat_axis=0, tiled=True)
    blocks = blocks.reshape(GROUP, COUNT, TILES, PAIRS, 128)
    asked.append(move(tie(both, blocks), 1, True, 0))

    mine, other, earlier = [], [], meta
    for i in range(COUNT):
        part = attend(i, meta, blocks, asked[i], selected.T, earlier)
        earlier = part
        mine.append(move(part, i, False, 0))
        other.append(lax.ppermute(mine[i], "head", swap))
    state = premerge(mine[0], other[0])
    return merge(meta, [state, mine[1], other[1]]).reshape(RDEV, 2 * HEADS * KL)


def solution(mesh):
    grid = Mesh(mesh.devices.reshape(NY, NK, 2, NX, 2), ("y", "zhi", "zlo", "x", "head"))
    seq = ("y", "zhi", "zlo", "x")
    placed = (P(seq, "head"), P(None, seq, None), P())
    return jax.shard_map(
        per_device, mesh=grid, in_specs=placed, out_specs=P(seq, None), check_vma=False
    )
```

```python
import functools

import jax
import jax.numpy as jnp
from jax import lax
from jax.experimental import pallas as pl
from jax.experimental.pallas import tpu as pltpu
from jax.sharding import Mesh
from jax.sharding import PartitionSpec as P

KL = 512
KR = 64
FEAT = KL + KR
WIDE = KL + 2 * KR
BLOCK = 64
PAIRS = BLOCK // 2
UNIT = PAIRS // 2
PAIR_WIDTH = 2 * FEAT
SPAN = UNIT * PAIR_WIDTH
TILES = PAIR_WIDTH // 128
TOPK = 32
RDEV = 2
BLK_DEV = 8
HEADS = 64
NY, NZ, NX = 4, 8, 4
NK = NZ // 2
GROUP = NY * 2 * NX
SEQ = NY * NZ * NX
ROWS = RDEV * HEADS
TAIL = 16
EMPTY = -1e30
MIB = 1024 * 1024

score_scale = 192.0 ** (-0.5)

COUNT = 2


def owner_place(zhi, zlo, core, i):
    if core == 0:
        return ((zhi + 2) % NK, 1 - zlo) if i == 0 else (zhi, zlo)
    return (zhi + 3 - 2 * zlo) % NK, zlo if i == 0 else 1 - zlo


def here():
    return tuple(lax.axis_index(name) for name in ("y", "zhi", "zlo", "x", "head"))


def pick_kernel(selected_ref, cache_ref, out_ref, held_ref, sems):
    steps = [(y, n) for y in range(NY) for n in range(COUNT)]
    y, zhi, zlo, x, core = here()
    pairs = [(zhi + jnp.where(core == 0, 2 - 2 * n, 3 - 2 * n)) % NK for n in range(COUNT)]

    def fetch(s):
        request = steps[s][0] * NK + pairs[steps[s][1]]
        return pltpu.make_async_copy(cache_ref.at[request], held_ref.at[s], sems.at[s])

    for s in range(len(steps)):
        fetch(s).start(priority=s % 2)
    me = ((y * NK + zhi) * 2 + zlo) * NX + x
    selected = selected_ref[...]
    inner = jnp.where((selected >> 3) == me, selected & (BLK_DEV - 1), -1)
    inner = jnp.max(inner, axis=0, keepdims=True)
    inner = jnp.maximum(inner, pltpu.roll(inner, SEQ * RDEV - 1, 1))
    row = lax.broadcasted_iota(jnp.int32, (2 * NX * UNIT, BLK_DEV * UNIT), 0)
    col = lax.broadcasted_iota(jnp.int32, (2 * NX * UNIT, BLK_DEV * UNIT), 1)
    token, held = (col >> 3) == (row & (UNIT - 1)), col & (BLK_DEV - 1)
    lane = lax.broadcasted_iota(jnp.int32, (2 * NX * UNIT, SEQ * RDEV), 1)
    slot = lax.broadcasted_iota(jnp.int32, (2 * NX * UNIT, SEQ * RDEV), 0) >> 4
    for s, (y, n) in enumerate(steps):
        base = (y * NK + pairs[n]) * (2 * NX)
        mine = lane == RDEV * (base + slot)
        block = jnp.sum(jnp.where(mine, inner, 0), axis=1, keepdims=True)
        onehot = jnp.where(token & (held == block), 1.0, 0.0).astype(jnp.bfloat16)
        fetch(s).wait()
        for half in range(2):
            pieces = [
                held_ref[s, :, p * PAIR_WIDTH : (p + 1) * PAIR_WIDTH].astype(jnp.float32)
                for p in range(half * UNIT, (half + 1) * UNIT)
            ]
            stacked = jnp.concatenate(pieces, axis=0).astype(jnp.bfloat16)
            picked = jnp.dot(onehot, stacked, preferred_element_type=jnp.float32)
            picked = picked.astype(jnp.bfloat16).reshape(2, NX, UNIT, PAIR_WIDTH)
            for zlo in range(2):
                chip = jnp.where(core == 0, 1 - zlo if n == 0 else zlo, n)
                index = jnp.where(core == 0, n, 0 if n == zlo else 1)
                span = slice(half * UNIT, (half + 1) * UNIT)
                for t in range(TILES):
                    tile = picked[zlo, :, :, t * 128 : (t + 1) * 128]
                    out_ref[y, pl.ds(chip * NX, NX), index, t, span] = tile


def pick_blocks(selected, cache):
    count = NY * COUNT
    return pl.pallas_call(
        pick_kernel,
        out_shape=jax.ShapeDtypeStruct((NY, 2 * NX, COUNT, TILES, PAIRS, 128), jnp.bfloat16),
        in_specs=[pl.BlockSpec(memory_space=pltpu.VMEM), pl.BlockSpec(memory_space=pl.ANY)],
        out_specs=pl.BlockSpec(memory_space=pltpu.VMEM),
        scratch_shapes=[
            pltpu.VMEM((count, BLK_DEV, BLOCK * FEAT), jnp.bfloat16),
            pltpu.SemaphoreType.DMA((count,)),
        ],
        compiler_params=pltpu.CompilerParams(vmem_limit_bytes=46 * MIB),
        name="pick_blocks",
    )(selected, cache)


def tie_kernel(*refs):
    pass


def tie(value, *earlier):
    anywhere = pl.BlockSpec(memory_space=pl.ANY)
    return pl.pallas_call(
        tie_kernel,
        out_shape=jax.ShapeDtypeStruct(value.shape, value.dtype),
        in_specs=[anywhere] * (1 + len(earlier)),
        out_specs=anywhere,
        input_output_aliases={0: 0},
        compiler_params=pltpu.CompilerParams(vmem_limit_bytes=MIB),
        name="tie",
    )(value, *earlier)


def spread_queries(packed):
    lane = lax.broadcasted_iota(jnp.int32, (RDEV * HEADS // 2, WIDE), 1)
    even = jnp.where(lane < FEAT, packed[:, :WIDE].astype(jnp.float32), 0.0)
    odd = jnp.where(lane >= KR, packed[:, KL:].astype(jnp.float32), 0.0)
    low = [even, pltpu.roll(odd, FEAT, 1)]
    high = [pltpu.roll(even, KR, 1), odd]
    return low, high


def attend_kernel(i, blocks_ref, selected_ref, _, *refs):
    width = GROUP * PAIRS
    pairs = jnp.concatenate(
        [blocks_ref[:, i, t].reshape(width, 128) for t in range(TILES)], axis=1
    )
    low, high = [], []
    views = [refs[0].at[0], refs[0].at[1]] if i else refs[:-1]
    for query_ref in views:
        parts = spread_queries(query_ref[...])
        low += parts[0]
        high += parts[1]
    query = jnp.concatenate(low, axis=0).astype(jnp.bfloat16)
    shifted = jnp.concatenate(high, axis=0).astype(jnp.bfloat16)
    out_ref = refs[-1]
    y, zhi, zlo, x, core = here()
    first, second = (owner_place(zhi, zlo, c, i) for c in range(2))
    pair = jnp.where(core == 0, first[0], second[0])
    chip = jnp.where(core == 0, first[1], second[1])
    owner = (y * NK + pair) * (2 * NX) + chip * NX + x
    slot = lax.broadcasted_iota(jnp.int32, (1, width), 1) >> 5
    holder = (slot >> 3) * (NK * 2 * NX) + (zhi * (2 * NX) + (slot & 7))
    places = selected_ref[...] >> 3
    lane = lax.broadcasted_iota(jnp.int32, places.shape, 1)
    rows = []
    for j in range(RDEV):
        mine = jnp.sum(jnp.where(lane == RDEV * owner + j, places, 0), axis=1, keepdims=True)
        read = jnp.max(jnp.where(mine == holder, 1.0, 0.0), axis=0, keepdims=True)
        rows.append(jnp.broadcast_to(read, (HEADS // 2, width)))
    valid = jnp.concatenate(rows * 4, axis=0) > 0.5
    dims = (((1,), (1,)), ((), ()))
    odd_keys = pairs[:, KL:]
    even = lax.dot_general(query, pairs[:, :WIDE], dims, preferred_element_type=jnp.float32)
    odd = lax.dot_general(shifted, odd_keys, dims, preferred_element_type=jnp.float32)
    even = jnp.where(valid, even * score_scale, EMPTY)
    odd = jnp.where(valid, odd * score_scale, EMPTY)
    top = jnp.max(jnp.maximum(even, odd), axis=1, keepdims=True)
    even = jnp.where(valid, jnp.exp(even - top), 0.0)
    odd = jnp.where(valid, jnp.exp(odd - top), 0.0)
    total = jnp.maximum(jnp.sum(even + odd, axis=1, keepdims=True), 1.0)
    value = jnp.dot(
        even.astype(jnp.bfloat16), pairs[:, :KL], preferred_element_type=jnp.float32
    )
    odd_value = jnp.dot(odd.astype(jnp.bfloat16), odd_keys, preferred_element_type=jnp.float32)
    value = (value + odd_value[:, KR : KR + KL]) * (1.0 / total)
    level = top + jnp.log(total)
    wide = jnp.transpose(jnp.broadcast_to(level, (2 * ROWS, 128)))[:TAIL]
    high = wide.astype(jnp.bfloat16).astype(jnp.float32)
    middle = (wide - high).astype(jnp.bfloat16).astype(jnp.float32)
    low = wide - high - middle
    line = lax.broadcasted_iota(jnp.int32, wide.shape, 0)
    tail = jnp.where(line == 0, high, jnp.where(line == 1, middle, jnp.where(line == 2, low, 0.0)))
    out_ref[: 2 * ROWS] = value.astype(jnp.bfloat16)
    out_ref[2 * ROWS :, : 2 * ROWS] = tail.astype(jnp.bfloat16)
    out_ref[2 * ROWS :, 2 * ROWS :] = jnp.zeros((TAIL, KL - 2 * ROWS), jnp.bfloat16)


def attend(i, blocks, selected, earlier, *queries):
    local = pl.BlockSpec(memory_space=pltpu.VMEM)
    return pl.pallas_call(
        functools.partial(attend_kernel, i),
        out_shape=jax.ShapeDtypeStruct((2 * ROWS + TAIL, KL), jnp.bfloat16),
        in_specs=[local, local, pl.BlockSpec(memory_space=pl.ANY)] + [local] * len(queries),
        out_specs=local,
        compiler_params=pltpu.CompilerParams(vmem_limit_bytes=24 * MIB),
        cost_estimate=pl.CostEstimate(flops=1, bytes_accessed=1, transcendentals=0),
        name="attend",
    )(blocks, selected, earlier, *queries)


def weigh(values, levels):
    peak = functools.reduce(jnp.maximum, levels)
    weights = [jnp.exp(level - peak) for level in levels]
    total = functools.reduce(jnp.add, weights)
    scale = 1.0 / total
    mean = jnp.zeros((ROWS, KL), jnp.float32)
    for value, weight in zip(values, weights):
        column = jnp.transpose(jnp.broadcast_to(weight * scale, (128, ROWS)))
        factor = jnp.concatenate([column] * (KL // 128), axis=1)
        mean = mean + factor * value.astype(jnp.float32)
    return mean, peak + jnp.log(total)


def halves_of(ref, half):
    tail = ref[2 * ROWS :, half * ROWS : (half + 1) * ROWS].astype(jnp.float32)
    return ref[half * ROWS : (half + 1) * ROWS], jnp.sum(tail, axis=0, keepdims=True)


def premerge_kernel(mine_ref, other_ref, out_ref):
    for half in range(2):
        views = [halves_of(mine_ref, half), halves_of(other_ref, 1 - half)]
        mean, level = weigh([view[0] for view in views], [view[1] for view in views])
        out_ref[half, :ROWS] = mean
        out_ref[half, ROWS:, :ROWS] = jnp.broadcast_to(level, (8, ROWS))
        out_ref[half, ROWS:, ROWS:] = jnp.zeros((8, KL - ROWS), jnp.float32)


def premerge(mine, other):
    return pl.pallas_call(
        premerge_kernel,
        out_shape=jax.ShapeDtypeStruct((2, ROWS + 8, KL), jnp.float32),
        compiler_params=pltpu.CompilerParams(vmem_limit_bytes=8 * MIB),
        name="premerge",
    )(mine, other)


def merge_kernel(state_ref, mine_ref, other_ref, out_ref):
    core = lax.axis_index("head")
    for half in range(2):
        state = (state_ref[half, :ROWS], state_ref[half, ROWS : ROWS + 1, :ROWS])
        views = [state, halves_of(mine_ref, half), halves_of(other_ref, 1 - half)]
        mean, _ = weigh([view[0] for view in views], [view[1] for view in views])
        mean = mean.astype(jnp.bfloat16).reshape(2, RDEV, HEADS // 2, KL)
        for odd in range(2):
            out_ref[:, core ^ half, :, odd * KL : (odd + 1) * KL] = mean[odd]


def merge(parts):
    return pl.pallas_call(
        merge_kernel,
        out_shape=jax.ShapeDtypeStruct((RDEV, 2, HEADS // 2, 2 * KL), jnp.bfloat16),
        compiler_params=pltpu.CompilerParams(vmem_limit_bytes=12 * MIB),
        name="merge",
    )(*parts)


def per_device(queries, cache, selected):
    def move(value, i, back, cross):
        pairs = []
        for zz in range(NZ):
            for c in range(2):
                pair, chip = owner_place(zz // 2, zz % 2, c, i)
                pairs.append((zz * 2 + c, (pair * 2 + chip) * 2 + (c ^ cross)))
        pairs = [pair[::-1] for pair in pairs] if back else pairs
        return lax.ppermute(value, ("zhi", "zlo", "head"), pairs)

    swap = [(0, 1), (1, 0)]
    packed = queries.reshape(ROWS // 2, PAIR_WIDTH)
    asked = [[move(packed, 0, True, cross) for cross in range(2)]]
    both = jnp.stack([packed, lax.ppermute(packed, "head", swap)])
    picked = tie(pick_blocks(selected.T, cache), *asked[0], both)
    picked = picked.reshape(GROUP, COUNT * TILES * PAIRS, 128)
    blocks = lax.all_to_all(picked, ("y", "zlo", "x"), split_axis=0, concat_axis=0, tiled=True)
    blocks = blocks.reshape(GROUP, COUNT, TILES, PAIRS, 128)
    asked.append([move(tie(both, blocks), 1, True, 0)])

    mine, other, earlier = [], [], packed
    for i in range(COUNT):
        part = attend(i, blocks, selected.T, earlier, *asked[i])
        earlier = part
        mine.append(move(part, i, False, 0))
        other.append(lax.ppermute(mine[i], "head", swap))
    state = premerge(mine[0], other[0])
    return merge([state, mine[1], other[1]]).reshape(RDEV, 2 * HEADS * KL)


def solution(mesh):
    grid = Mesh(mesh.devices.reshape(NY, NK, 2, NX, 2), ("y", "zhi", "zlo", "x", "head"))
    seq = ("y", "zhi", "zlo", "x")
    placed = (P(seq, "head"), P(None, seq, None), P())
    return jax.shard_map(
        per_device, mesh=grid, in_specs=placed, out_specs=P(seq, None), check_vma=False
    )
```

```python
import functools

import jax
import jax.numpy as jnp
from jax import lax
from jax.experimental import pallas as pl
from jax.experimental.pallas import tpu as pltpu
from jax.sharding import Mesh
from jax.sharding import PartitionSpec as P

KL = 512
KR = 64
FEAT = KL + KR
WIDE = KL + 2 * KR
BLOCK = 64
PAIRS = BLOCK // 2
UNIT = PAIRS // 2
PAIR_WIDTH = 2 * FEAT
SPAN = UNIT * PAIR_WIDTH
TILES = PAIR_WIDTH // 128
TOPK = 32
RDEV = 2
BLK_DEV = 8
HEADS = 64
NY, NZ, NX = 4, 8, 4
NK = NZ // 2
GROUP = NY * 2 * NX
SEQ = NY * NZ * NX
ROWS = RDEV * HEADS
TAIL = 16
EMPTY = -1e30
MIB = 1024 * 1024

score_scale = 192.0 ** (-0.5)

COUNT = 2


def owner_place(zhi, zlo, core, i):
    if core == 0:
        return ((zhi + 2) % NK, 1 - zlo) if i == 0 else (zhi, zlo)
    return (zhi + 3 - 2 * zlo) % NK, zlo if i == 0 else 1 - zlo


def here():
    return tuple(lax.axis_index(name) for name in ("y", "zhi", "zlo", "x", "head"))


def pick_kernel(
    selected_ref, cache_ref, packed_ref, swapped_ref, out_ref, both_ref, held_ref, table_ref, sems
):
    steps = [(y, n) for y in range(NY) for n in range(COUNT)]
    y, zhi, zlo, x, core = here()
    pairs = [(zhi + jnp.where(core == 0, 2 - 2 * n, 3 - 2 * n)) % NK for n in range(COUNT)]

    def fetch(s):
        request = steps[s][0] * NK + pairs[steps[s][1]]
        return pltpu.make_async_copy(cache_ref.at[request], held_ref.at[s], sems.at[s])

    table = pltpu.make_async_copy(selected_ref, table_ref, sems.at[len(steps)])
    table.start(priority=1)
    for s in range(len(steps)):
        fetch(s).start(priority=s % 2)
    both_ref[0] = packed_ref[...]
    both_ref[1] = swapped_ref[...]
    table.wait()
    me = ((y * NK + zhi) * 2 + zlo) * NX + x
    selected = table_ref[...]
    inner = jnp.where((selected >> 3) == me, selected & (BLK_DEV - 1), -1)
    inner = jnp.max(inner, axis=0, keepdims=True)
    inner = jnp.maximum(inner, pltpu.roll(inner, SEQ * RDEV - 1, 1))
    row = lax.broadcasted_iota(jnp.int32, (2 * NX * UNIT, BLK_DEV * UNIT), 0)
    col = lax.broadcasted_iota(jnp.int32, (2 * NX * UNIT, BLK_DEV * UNIT), 1)
    token, held = (col >> 3) == (row & (UNIT - 1)), col & (BLK_DEV - 1)
    lane = lax.broadcasted_iota(jnp.int32, (2 * NX * UNIT, SEQ * RDEV), 1)
    slot = lax.broadcasted_iota(jnp.int32, (2 * NX * UNIT, SEQ * RDEV), 0) >> 4
    for s, (y, n) in enumerate(steps):
        base = (y * NK + pairs[n]) * (2 * NX)
        mine = lane == RDEV * (base + slot)
        block = jnp.sum(jnp.where(mine, inner, 0), axis=1, keepdims=True)
        onehot = jnp.where(token & (held == block), 1.0, 0.0).astype(jnp.bfloat16)
        fetch(s).wait()
        for half in range(2):
            pieces = [
                held_ref[s, :, p * PAIR_WIDTH : (p + 1) * PAIR_WIDTH].astype(jnp.float32)
                for p in range(half * UNIT, (half + 1) * UNIT)
            ]
            stacked = jnp.concatenate(pieces, axis=0).astype(jnp.bfloat16)
            picked = jnp.dot(onehot, stacked, preferred_element_type=jnp.float32)
            picked = picked.astype(jnp.bfloat16).reshape(2, NX, UNIT, PAIR_WIDTH)
            for zlo in range(2):
                chip = jnp.where(core == 0, 1 - zlo if n == 0 else zlo, n)
                index = jnp.where(core == 0, n, 0 if n == zlo else 1)
                span = slice(half * UNIT, (half + 1) * UNIT)
                for t in range(TILES):
                    tile = picked[zlo, :, :, t * 128 : (t + 1) * 128]
                    out_ref[y, pl.ds(chip * NX, NX), index, t, span] = tile


def pick_blocks(selected, cache, packed, swapped):
    count = NY * COUNT
    local, anywhere = (pl.BlockSpec(memory_space=space) for space in (pltpu.VMEM, pl.ANY))
    return pl.pallas_call(
        pick_kernel,
        out_shape=[
            jax.ShapeDtypeStruct((NY, 2 * NX, COUNT, TILES, PAIRS, 128), jnp.bfloat16),
            jax.ShapeDtypeStruct((2,) + packed.shape, jnp.bfloat16),
        ],
        in_specs=[anywhere, anywhere, local, local],
        out_specs=[local, local],
        scratch_shapes=[
            pltpu.VMEM((count, BLK_DEV, BLOCK * FEAT), jnp.bfloat16),
            pltpu.VMEM(selected.shape, jnp.int32),
            pltpu.SemaphoreType.DMA((count + 1,)),
        ],
        compiler_params=pltpu.CompilerParams(vmem_limit_bytes=46 * MIB),
        name="pick_blocks",
    )(selected, cache, packed, swapped)


def tie_kernel(*refs):
    pass


def tie(value, *earlier):
    anywhere = pl.BlockSpec(memory_space=pl.ANY)
    return pl.pallas_call(
        tie_kernel,
        out_shape=jax.ShapeDtypeStruct(value.shape, value.dtype),
        in_specs=[anywhere] * (1 + len(earlier)),
        out_specs=anywhere,
        input_output_aliases={0: 0},
        compiler_params=pltpu.CompilerParams(vmem_limit_bytes=MIB),
        name="tie",
    )(value, *earlier)


def spread_queries(packed):
    lane = lax.broadcasted_iota(jnp.int32, (RDEV * HEADS // 2, WIDE), 1)
    even = jnp.where(lane < FEAT, packed[:, :WIDE].astype(jnp.float32), 0.0)
    odd = jnp.where(lane >= KR, packed[:, KL:].astype(jnp.float32), 0.0)
    low = [even, pltpu.roll(odd, FEAT, 1)]
    high = [pltpu.roll(even, KR, 1), odd]
    return low, high


def attend_kernel(i, blocks_ref, selected_ref, _, *refs):
    width = GROUP * PAIRS
    pairs = jnp.concatenate(
        [blocks_ref[:, i, t].reshape(width, 128) for t in range(TILES)], axis=1
    )
    low, high = [], []
    views = [refs[0].at[0], refs[0].at[1]] if i else refs[:-1]
    for query_ref in views:
        parts = spread_queries(query_ref[...])
        low += parts[0]
        high += parts[1]
    query = jnp.concatenate(low, axis=0).astype(jnp.bfloat16)
    shifted = jnp.concatenate(high, axis=0).astype(jnp.bfloat16)
    out_ref = refs[-1]
    y, zhi, zlo, x, core = here()
    first, second = (owner_place(zhi, zlo, c, i) for c in range(2))
    pair = jnp.where(core == 0, first[0], second[0])
    chip = jnp.where(core == 0, first[1], second[1])
    owner = (y * NK + pair) * (2 * NX) + chip * NX + x
    slot = lax.broadcasted_iota(jnp.int32, (1, width), 1) >> 5
    holder = (slot >> 3) * (NK * 2 * NX) + (zhi * (2 * NX) + (slot & 7))
    places = selected_ref[...] >> 3
    lane = lax.broadcasted_iota(jnp.int32, places.shape, 1)
    rows = []
    for j in range(RDEV):
        mine = jnp.sum(jnp.where(lane == RDEV * owner + j, places, 0), axis=1, keepdims=True)
        read = jnp.max(jnp.where(mine == holder, 1.0, 0.0), axis=0, keepdims=True)
        rows.append(jnp.broadcast_to(read, (HEADS // 2, width)))
    valid = jnp.concatenate(rows * 4, axis=0) > 0.5
    dims = (((1,), (1,)), ((), ()))
    odd_keys = pairs[:, KL:]
    even = lax.dot_general(query, pairs[:, :WIDE], dims, preferred_element_type=jnp.float32)
    odd = lax.dot_general(shifted, odd_keys, dims, preferred_element_type=jnp.float32)
    even = jnp.where(valid, even * score_scale, EMPTY)
    odd = jnp.where(valid, odd * score_scale, EMPTY)
    top = jnp.max(jnp.maximum(even, odd), axis=1, keepdims=True)
    even = jnp.exp(even - top)
    odd = jnp.exp(odd - top)
    total = jnp.sum(even + odd, axis=1, keepdims=True)
    value = jnp.dot(
        even.astype(jnp.bfloat16), pairs[:, :KL], preferred_element_type=jnp.float32
    )
    odd_value = jnp.dot(odd.astype(jnp.bfloat16), odd_keys, preferred_element_type=jnp.float32)
    value = (value + odd_value[:, KR : KR + KL]) * (1.0 / total)
    level = top + jnp.log(total)
    wide = jnp.transpose(jnp.broadcast_to(level, (2 * ROWS, 128)))[:TAIL]
    high = wide.astype(jnp.bfloat16).astype(jnp.float32)
    middle = (wide - high).astype(jnp.bfloat16).astype(jnp.float32)
    low = wide - high - middle
    line = lax.broadcasted_iota(jnp.int32, wide.shape, 0)
    tail = jnp.where(line == 0, high, jnp.where(line == 1, middle, jnp.where(line == 2, low, 0.0)))
    out_ref[: 2 * ROWS] = value.astype(jnp.bfloat16)
    out_ref[2 * ROWS :, : 2 * ROWS] = tail.astype(jnp.bfloat16)
    out_ref[2 * ROWS :, 2 * ROWS :] = jnp.zeros((TAIL, KL - 2 * ROWS), jnp.bfloat16)


def attend(i, blocks, selected, earlier, *queries):
    local = pl.BlockSpec(memory_space=pltpu.VMEM)
    return pl.pallas_call(
        functools.partial(attend_kernel, i),
        out_shape=jax.ShapeDtypeStruct((2 * ROWS + TAIL, KL), jnp.bfloat16),
        in_specs=[local, local, pl.BlockSpec(memory_space=pl.ANY)] + [local] * len(queries),
        out_specs=local,
        compiler_params=pltpu.CompilerParams(vmem_limit_bytes=24 * MIB),
        cost_estimate=pl.CostEstimate(flops=1, bytes_accessed=1, transcendentals=0),
        name="attend",
    )(blocks, selected, earlier, *queries)


def weigh(values, levels):
    peak = functools.reduce(jnp.maximum, levels)
    weights = [jnp.exp(level - peak) for level in levels]
    total = functools.reduce(jnp.add, weights)
    scale = 1.0 / total
    mean = jnp.zeros((ROWS, KL), jnp.float32)
    for value, weight in zip(values, weights):
        column = jnp.transpose(jnp.broadcast_to(weight * scale, (128, ROWS)))
        factor = jnp.concatenate([column] * (KL // 128), axis=1)
        mean = mean + factor * value.astype(jnp.float32)
    return mean, peak + jnp.log(total)


def halves_of(ref, half):
    tail = ref[2 * ROWS :, half * ROWS : (half + 1) * ROWS].astype(jnp.float32)
    return ref[half * ROWS : (half + 1) * ROWS], jnp.sum(tail, axis=0, keepdims=True)


def premerge_kernel(mine_ref, other_ref, out_ref):
    for half in range(2):
        views = [halves_of(mine_ref, half), halves_of(other_ref, 1 - half)]
        mean, level = weigh([view[0] for view in views], [view[1] for view in views])
        out_ref[half, :ROWS] = mean
        out_ref[half, ROWS:, :ROWS] = jnp.broadcast_to(level, (8, ROWS))
        out_ref[half, ROWS:, ROWS:] = jnp.zeros((8, KL - ROWS), jnp.float32)


def premerge(mine, other):
    return pl.pallas_call(
        premerge_kernel,
        out_shape=jax.ShapeDtypeStruct((2, ROWS + 8, KL), jnp.float32),
        compiler_params=pltpu.CompilerParams(vmem_limit_bytes=8 * MIB),
        name="premerge",
    )(mine, other)


def merge_kernel(state_ref, mine_ref, other_ref, out_ref):
    core = lax.axis_index("head")
    for half in range(2):
        state = (state_ref[half, :ROWS], state_ref[half, ROWS : ROWS + 1, :ROWS])
        views = [state, halves_of(mine_ref, half), halves_of(other_ref, 1 - half)]
        mean, _ = weigh([view[0] for view in views], [view[1] for view in views])
        mean = mean.astype(jnp.bfloat16).reshape(2, RDEV, HEADS // 2, KL)
        for odd in range(2):
            out_ref[:, core ^ half, :, odd * KL : (odd + 1) * KL] = mean[odd]


def merge(parts):
    return pl.pallas_call(
        merge_kernel,
        out_shape=jax.ShapeDtypeStruct((RDEV, 2, HEADS // 2, 2 * KL), jnp.bfloat16),
        compiler_params=pltpu.CompilerParams(vmem_limit_bytes=12 * MIB),
        name="merge",
    )(*parts)


def per_device(queries, cache, selected):
    def move(value, i, back, cross):
        pairs = []
        for zz in range(NZ):
            for c in range(2):
                pair, chip = owner_place(zz // 2, zz % 2, c, i)
                pairs.append((zz * 2 + c, (pair * 2 + chip) * 2 + (c ^ cross)))
        pairs = [pair[::-1] for pair in pairs] if back else pairs
        return lax.ppermute(value, ("zhi", "zlo", "head"), pairs)

    swap = [(0, 1), (1, 0)]
    packed = queries.reshape(ROWS // 2, PAIR_WIDTH)
    asked = [[move(packed, 0, True, cross) for cross in range(2)]]
    picked, both = pick_blocks(selected.T, cache, packed, lax.ppermute(packed, "head", swap))
    picked = tie(picked, *asked[0])
    picked = picked.reshape(GROUP, COUNT * TILES * PAIRS, 128)
    blocks = lax.all_to_all(picked, ("y", "zlo", "x"), split_axis=0, concat_axis=0, tiled=True)
    blocks = blocks.reshape(GROUP, COUNT, TILES, PAIRS, 128)
    asked.append([move(tie(both, blocks), 1, True, 0)])

    mine, other, earlier = [], [], packed
    for i in range(COUNT):
        part = attend(i, blocks, selected.T, earlier, *asked[i])
        earlier = part
        mine.append(move(part, i, False, 0))
        other.append(lax.ppermute(mine[i], "head", swap))
    state = premerge(mine[0], other[0])
    return merge([state, mine[1], other[1]]).reshape(RDEV, 2 * HEADS * KL)


def solution(mesh):
    grid = Mesh(mesh.devices.reshape(NY, NK, 2, NX, 2), ("y", "zhi", "zlo", "x", "head"))
    seq = ("y", "zhi", "zlo", "x")
    placed = (P(seq, "head"), P(None, seq, None), P())
    return jax.shard_map(
        per_device, mesh=grid, in_specs=placed, out_specs=P(seq, None), check_vma=False
    )
```

```python
import functools

import jax
import jax.numpy as jnp
from jax import lax
from jax.experimental import pallas as pl
from jax.experimental.pallas import tpu as pltpu
from jax.sharding import Mesh
from jax.sharding import PartitionSpec as P

KL = 512
KR = 64
FEAT = KL + KR
WIDE = KL + 2 * KR
BLOCK = 64
PAIRS = BLOCK // 2
UNIT = PAIRS // 2
PAIR_WIDTH = 2 * FEAT
SPAN = UNIT * PAIR_WIDTH
TILES = PAIR_WIDTH // 128
TOPK = 32
RDEV = 2
BLK_DEV = 8
HEADS = 64
NY, NZ, NX = 4, 8, 4
NK = NZ // 2
GROUP = NY * 2 * NX
SEQ = NY * NZ * NX
ROWS = RDEV * HEADS
TAIL = 16
EMPTY = -1e30
MIB = 1024 * 1024

score_scale = 192.0 ** (-0.5)

COUNT = 2


def owner_place(zhi, zlo, core, i):
    if core == 0:
        return ((zhi + 2) % NK, 1 - zlo) if i == 0 else (zhi, zlo)
    return (zhi + 3 - 2 * zlo) % NK, zlo if i == 0 else 1 - zlo


def here():
    return tuple(lax.axis_index(name) for name in ("y", "zhi", "zlo", "x", "head"))


def pick_kernel(selected_ref, cache_ref, out_ref, held_ref, sems):
    steps = [(y, n) for y in range(NY) for n in range(COUNT)]
    y, zhi, zlo, x, core = here()
    pairs = [(zhi + jnp.where(core == 0, 2 - 2 * n, 3 - 2 * n)) % NK for n in range(COUNT)]

    def fetch(s):
        request = steps[s][0] * NK + pairs[steps[s][1]]
        return pltpu.make_async_copy(cache_ref.at[request], held_ref.at[s], sems.at[s])

    for s in range(len(steps)):
        fetch(s).start(priority=s % 2)
    me = ((y * NK + zhi) * 2 + zlo) * NX + x
    selected = selected_ref[...]
    inner = jnp.where((selected >> 3) == me, selected & (BLK_DEV - 1), -1)
    inner = jnp.max(inner, axis=0, keepdims=True)
    inner = jnp.maximum(inner, pltpu.roll(inner, SEQ * RDEV - 1, 1))
    row = lax.broadcasted_iota(jnp.int32, (2 * NX * UNIT, BLK_DEV * UNIT), 0)
    col = lax.broadcasted_iota(jnp.int32, (2 * NX * UNIT, BLK_DEV * UNIT), 1)
    token, held = (col >> 3) == (row & (UNIT - 1)), col & (BLK_DEV - 1)
    lane = lax.broadcasted_iota(jnp.int32, (2 * NX * UNIT, SEQ * RDEV), 1)
    slot = lax.broadcasted_iota(jnp.int32, (2 * NX * UNIT, SEQ * RDEV), 0) >> 4
    for s, (y, n) in enumerate(steps):
        base = (y * NK + pairs[n]) * (2 * NX)
        mine = lane == RDEV * (base + slot)
        block = jnp.sum(jnp.where(mine, inner, 0), axis=1, keepdims=True)
        onehot = jnp.where(token & (held == block), 1.0, 0.0).astype(jnp.bfloat16)
        fetch(s).wait()
        for half in range(2):
            pieces = [
                held_ref[s, :, p * PAIR_WIDTH : (p + 1) * PAIR_WIDTH].astype(jnp.float32)
                for p in range(half * UNIT, (half + 1) * UNIT)
            ]
            stacked = jnp.concatenate(pieces, axis=0).astype(jnp.bfloat16)
            picked = jnp.dot(onehot, stacked, preferred_element_type=jnp.float32)
            picked = picked.astype(jnp.bfloat16).reshape(2, NX, UNIT, PAIR_WIDTH)
            for zlo in range(2):
                chip = jnp.where(core == 0, 1 - zlo if n == 0 else zlo, n)
                index = jnp.where(core == 0, n, 0 if n == zlo else 1)
                span = slice(half * UNIT, (half + 1) * UNIT)
                for t in range(TILES):
                    tile = picked[zlo, :, :, t * 128 : (t + 1) * 128]
                    out_ref[:, chip, y, index, t, span] = tile


def pick_blocks(selected, cache):
    count = NY * COUNT
    return pl.pallas_call(
        pick_kernel,
        out_shape=jax.ShapeDtypeStruct((NX, 2, NY, COUNT, TILES, PAIRS, 128), jnp.bfloat16),
        in_specs=[pl.BlockSpec(memory_space=pltpu.VMEM), pl.BlockSpec(memory_space=pl.ANY)],
        out_specs=pl.BlockSpec(memory_space=pltpu.VMEM),
        scratch_shapes=[
            pltpu.VMEM((count, BLK_DEV, BLOCK * FEAT), jnp.bfloat16),
            pltpu.SemaphoreType.DMA((count,)),
        ],
        compiler_params=pltpu.CompilerParams(vmem_limit_bytes=46 * MIB),
        name="pick_blocks",
    )(selected, cache)


def tie_kernel(*refs):
    pass


def tie(value, *earlier):
    anywhere = pl.BlockSpec(memory_space=pl.ANY)
    return pl.pallas_call(
        tie_kernel,
        out_shape=jax.ShapeDtypeStruct(value.shape, value.dtype),
        in_specs=[anywhere] * (1 + len(earlier)),
        out_specs=anywhere,
        input_output_aliases={0: 0},
        compiler_params=pltpu.CompilerParams(vmem_limit_bytes=MIB),
        name="tie",
    )(value, *earlier)


def spread_queries(packed):
    lane = lax.broadcasted_iota(jnp.int32, (RDEV * HEADS // 2, WIDE), 1)
    even = jnp.where(lane < FEAT, packed[:, :WIDE].astype(jnp.float32), 0.0)
    odd = jnp.where(lane >= KR, packed[:, KL:].astype(jnp.float32), 0.0)
    low = [even, pltpu.roll(odd, FEAT, 1)]
    high = [pltpu.roll(even, KR, 1), odd]
    return low, high


def attend_kernel(i, blocks_ref, selected_ref, _, *refs):
    width = GROUP * PAIRS
    pairs = jnp.concatenate(
        [blocks_ref[:, i, t].reshape(width, 128) for t in range(TILES)], axis=1
    )
    low, high = [], []
    views = [refs[0].at[0], refs[0].at[1]] if i else refs[:-1]
    for query_ref in views:
        parts = spread_queries(query_ref[...])
        low += parts[0]
        high += parts[1]
    query = jnp.concatenate(low, axis=0).astype(jnp.bfloat16)
    shifted = jnp.concatenate(high, axis=0).astype(jnp.bfloat16)
    out_ref = refs[-1]
    y, zhi, zlo, x, core = here()
    first, second = (owner_place(zhi, zlo, c, i) for c in range(2))
    pair = jnp.where(core == 0, first[0], second[0])
    chip = jnp.where(core == 0, first[1], second[1])
    owner = (y * NK + pair) * (2 * NX) + chip * NX + x
    slot = lax.broadcasted_iota(jnp.int32, (1, width), 1) >> 5
    holder = (slot & 3) * (NK * 2 * NX) + (zhi * (2 * NX) + ((slot >> 2) & 1) * NX + (slot >> 3))
    places = selected_ref[...] >> 3
    lane = lax.broadcasted_iota(jnp.int32, places.shape, 1)
    rows = []
    for j in range(RDEV):
        mine = jnp.sum(jnp.where(lane == RDEV * owner + j, places, 0), axis=1, keepdims=True)
        read = jnp.max(jnp.where(mine == holder, 1.0, 0.0), axis=0, keepdims=True)
        rows.append(jnp.broadcast_to(read, (HEADS // 2, width)))
    valid = jnp.concatenate(rows * 4, axis=0) > 0.5
    dims = (((1,), (1,)), ((), ()))
    odd_keys = pairs[:, KL:]
    even = lax.dot_general(query, pairs[:, :WIDE], dims, preferred_element_type=jnp.float32)
    odd = lax.dot_general(shifted, odd_keys, dims, preferred_element_type=jnp.float32)
    even = jnp.where(valid, even * score_scale, EMPTY)
    odd = jnp.where(valid, odd * score_scale, EMPTY)
    top = jnp.max(jnp.maximum(even, odd), axis=1, keepdims=True)
    even = jnp.where(valid, jnp.exp(even - top), 0.0)
    odd = jnp.where(valid, jnp.exp(odd - top), 0.0)
    total = jnp.maximum(jnp.sum(even + odd, axis=1, keepdims=True), 1.0)
    value = jnp.dot(
        even.astype(jnp.bfloat16), pairs[:, :KL], preferred_element_type=jnp.float32
    )
    odd_value = jnp.dot(odd.astype(jnp.bfloat16), odd_keys, preferred_element_type=jnp.float32)
    value = (value + odd_value[:, KR : KR + KL]) * (1.0 / total)
    level = top + jnp.log(total)
    wide = jnp.transpose(jnp.broadcast_to(level, (2 * ROWS, 128)))[:TAIL]
    high = wide.astype(jnp.bfloat16).astype(jnp.float32)
    middle = (wide - high).astype(jnp.bfloat16).astype(jnp.float32)
    low = wide - high - middle
    line = lax.broadcasted_iota(jnp.int32, wide.shape, 0)
    tail = jnp.where(line == 0, high, jnp.where(line == 1, middle, jnp.where(line == 2, low, 0.0)))
    out_ref[: 2 * ROWS] = value.astype(jnp.bfloat16)
    out_ref[2 * ROWS :, : 2 * ROWS] = tail.astype(jnp.bfloat16)
    out_ref[2 * ROWS :, 2 * ROWS :] = jnp.zeros((TAIL, KL - 2 * ROWS), jnp.bfloat16)


def attend(i, blocks, selected, earlier, *queries):
    local = pl.BlockSpec(memory_space=pltpu.VMEM)
    return pl.pallas_call(
        functools.partial(attend_kernel, i),
        out_shape=jax.ShapeDtypeStruct((2 * ROWS + TAIL, KL), jnp.bfloat16),
        in_specs=[local, local, pl.BlockSpec(memory_space=pl.ANY)] + [local] * len(queries),
        out_specs=local,
        compiler_params=pltpu.CompilerParams(vmem_limit_bytes=24 * MIB),
        cost_estimate=pl.CostEstimate(flops=1, bytes_accessed=1, transcendentals=0),
        name="attend",
    )(blocks, selected, earlier, *queries)


def weigh(values, levels):
    peak = functools.reduce(jnp.maximum, levels)
    weights = [jnp.exp(level - peak) for level in levels]
    total = functools.reduce(jnp.add, weights)
    scale = 1.0 / total
    mean = jnp.zeros((ROWS, KL), jnp.float32)
    for value, weight in zip(values, weights):
        column = jnp.transpose(jnp.broadcast_to(weight * scale, (128, ROWS)))
        factor = jnp.concatenate([column] * (KL // 128), axis=1)
        mean = mean + factor * value.astype(jnp.float32)
    return mean, peak + jnp.log(total)


def halves_of(ref, half):
    tail = ref[2 * ROWS :, half * ROWS : (half + 1) * ROWS].astype(jnp.float32)
    return ref[half * ROWS : (half + 1) * ROWS], jnp.sum(tail, axis=0, keepdims=True)


def premerge_kernel(mine_ref, other_ref, out_ref):
    for half in range(2):
        views = [halves_of(mine_ref, half), halves_of(other_ref, 1 - half)]
        mean, level = weigh([view[0] for view in views], [view[1] for view in views])
        out_ref[half, :ROWS] = mean
        out_ref[half, ROWS:, :ROWS] = jnp.broadcast_to(level, (8, ROWS))
        out_ref[half, ROWS:, ROWS:] = jnp.zeros((8, KL - ROWS), jnp.float32)


def premerge(mine, other):
    return pl.pallas_call(
        premerge_kernel,
        out_shape=jax.ShapeDtypeStruct((2, ROWS + 8, KL), jnp.float32),
        compiler_params=pltpu.CompilerParams(vmem_limit_bytes=8 * MIB),
        name="premerge",
    )(mine, other)


def merge_kernel(state_ref, mine_ref, other_ref, out_ref):
    core = lax.axis_index("head")
    for half in range(2):
        state = (state_ref[half, :ROWS], state_ref[half, ROWS : ROWS + 1, :ROWS])
        views = [state, halves_of(mine_ref, half), halves_of(other_ref, 1 - half)]
        mean, _ = weigh([view[0] for view in views], [view[1] for view in views])
        mean = mean.astype(jnp.bfloat16).reshape(2, RDEV, HEADS // 2, KL)
        for odd in range(2):
            out_ref[:, core ^ half, :, odd * KL : (odd + 1) * KL] = mean[odd]


def merge(parts):
    return pl.pallas_call(
        merge_kernel,
        out_shape=jax.ShapeDtypeStruct((RDEV, 2, HEADS // 2, 2 * KL), jnp.bfloat16),
        compiler_params=pltpu.CompilerParams(vmem_limit_bytes=12 * MIB),
        name="merge",
    )(*parts)


def per_device(queries, cache, selected):
    def move(value, i, back, cross):
        pairs = []
        for zz in range(NZ):
            for c in range(2):
                pair, chip = owner_place(zz // 2, zz % 2, c, i)
                pairs.append((zz * 2 + c, (pair * 2 + chip) * 2 + (c ^ cross)))
        pairs = [pair[::-1] for pair in pairs] if back else pairs
        return lax.ppermute(value, ("zhi", "zlo", "head"), pairs)

    swap = [(0, 1), (1, 0)]
    packed = queries.reshape(ROWS // 2, PAIR_WIDTH)
    asked = [[move(packed, 0, True, cross) for cross in range(2)]]
    both = jnp.stack([packed, lax.ppermute(packed, "head", swap)])
    picked = tie(pick_blocks(selected.T, cache), *asked[0], both)
    picked = picked.reshape(GROUP, COUNT * TILES * PAIRS, 128)
    blocks = lax.all_to_all(picked, ("x", "zlo", "y"), split_axis=0, concat_axis=0, tiled=True)
    blocks = blocks.reshape(GROUP, COUNT, TILES, PAIRS, 128)
    asked.append([move(tie(both, blocks), 1, True, 0)])

    mine, other, earlier = [], [], packed
    for i in range(COUNT):
        part = attend(i, blocks, selected.T, earlier, *asked[i])
        earlier = part
        mine.append(move(part, i, False, 0))
        other.append(lax.ppermute(mine[i], "head", swap))
    state = premerge(mine[0], other[0])
    return merge([state, mine[1], other[1]]).reshape(RDEV, 2 * HEADS * KL)


def solution(mesh):
    grid = Mesh(mesh.devices.reshape(NY, NK, 2, NX, 2), ("y", "zhi", "zlo", "x", "head"))
    seq = ("y", "zhi", "zlo", "x")
    placed = (P(seq, "head"), P(None, seq, None), P())
    return jax.shard_map(
        per_device, mesh=grid, in_specs=placed, out_specs=P(seq, None), check_vma=False
    )
```

```python
import functools

import jax
import jax.numpy as jnp
from jax import lax
from jax.experimental import pallas as pl
from jax.experimental.pallas import tpu as pltpu
from jax.sharding import Mesh
from jax.sharding import PartitionSpec as P

KL = 512
KR = 64
FEAT = KL + KR
WIDE = KL + 2 * KR
BLOCK = 64
PAIRS = BLOCK // 2
UNIT = PAIRS // 2
PAIR_WIDTH = 2 * FEAT
SPAN = UNIT * PAIR_WIDTH
TILES = PAIR_WIDTH // 128
TOPK = 32
RDEV = 2
BLK_DEV = 8
HEADS = 64
NY, NZ, NX = 4, 8, 4
NK = NZ // 2
GROUP = NY * 2 * NX
SEQ = NY * NZ * NX
ROWS = RDEV * HEADS
TAIL = 16
EMPTY = -1e30
MIB = 1024 * 1024

score_scale = 192.0 ** (-0.5)

COUNT = 2


def owner_place(zhi, zlo, core, i):
    if core == 0:
        return ((zhi + 2) % NK, 1 - zlo) if i == 0 else (zhi, zlo)
    return (zhi + 3 - 2 * zlo) % NK, zlo if i == 0 else 1 - zlo


def here():
    return tuple(lax.axis_index(name) for name in ("y", "zhi", "zlo", "x", "head"))


def pick_kernel(
    selected_ref, cache_ref, packed_ref, swapped_ref, out_ref, both_ref, held_ref, table_ref, sems
):
    steps = [(y, n) for y in range(NY) for n in range(COUNT)]
    y, zhi, zlo, x, core = here()
    pairs = [(zhi + jnp.where(core == 0, 2 - 2 * n, 3 - 2 * n)) % NK for n in range(COUNT)]

    def fetch(s):
        request = steps[s][0] * NK + pairs[steps[s][1]]
        return pltpu.make_async_copy(cache_ref.at[request], held_ref.at[s], sems.at[s])

    table = pltpu.make_async_copy(selected_ref, table_ref, sems.at[len(steps)])
    table.start(priority=1)
    for s in range(len(steps)):
        fetch(s).start(priority=s % 2)
    both_ref[0] = packed_ref[...]
    both_ref[1] = swapped_ref[...]
    table.wait()
    me = ((y * NK + zhi) * 2 + zlo) * NX + x
    selected = table_ref[...]
    inner = jnp.where((selected >> 3) == me, selected & (BLK_DEV - 1), -1)
    inner = jnp.max(inner, axis=0, keepdims=True)
    inner = jnp.maximum(inner, pltpu.roll(inner, SEQ * RDEV - 1, 1))
    row = lax.broadcasted_iota(jnp.int32, (2 * NX * UNIT, BLK_DEV * UNIT), 0)
    col = lax.broadcasted_iota(jnp.int32, (2 * NX * UNIT, BLK_DEV * UNIT), 1)
    token, held = (col >> 3) == (row & (UNIT - 1)), col & (BLK_DEV - 1)
    lane = lax.broadcasted_iota(jnp.int32, (2 * NX * UNIT, SEQ * RDEV), 1)
    slot = lax.broadcasted_iota(jnp.int32, (2 * NX * UNIT, SEQ * RDEV), 0) >> 4
    for s, (y, n) in enumerate(steps):
        base = (y * NK + pairs[n]) * (2 * NX)
        mine = lane == RDEV * (base + slot)
        block = jnp.sum(jnp.where(mine, inner, 0), axis=1, keepdims=True)
        onehot = jnp.where(token & (held == block), 1.0, 0.0).astype(jnp.bfloat16)
        fetch(s).wait()
        for half in range(2):
            pieces = [
                held_ref[s, :, p * PAIR_WIDTH : (p + 1) * PAIR_WIDTH].astype(jnp.float32)
                for p in range(half * UNIT, (half + 1) * UNIT)
            ]
            stacked = jnp.concatenate(pieces, axis=0).astype(jnp.bfloat16)
            picked = jnp.dot(onehot, stacked, preferred_element_type=jnp.float32)
            picked = picked.astype(jnp.bfloat16).reshape(2, NX, UNIT, PAIR_WIDTH)
            for zlo in range(2):
                chip = jnp.where(core == 0, 1 - zlo if n == 0 else zlo, n)
                index = jnp.where(core == 0, n, 0 if n == zlo else 1)
                span = slice(half * UNIT, (half + 1) * UNIT)
                for t in range(TILES):
                    tile = picked[zlo, :, :, t * 128 : (t + 1) * 128]
                    out_ref[:, chip, y, index, t, span] = tile


def pick_blocks(selected, cache, packed, swapped):
    count = NY * COUNT
    local, anywhere = (pl.BlockSpec(memory_space=space) for space in (pltpu.VMEM, pl.ANY))
    return pl.pallas_call(
        pick_kernel,
        out_shape=[
            jax.ShapeDtypeStruct((NX, 2, NY, COUNT, TILES, PAIRS, 128), jnp.bfloat16),
            jax.ShapeDtypeStruct((2,) + packed.shape, jnp.bfloat16),
        ],
        in_specs=[anywhere, anywhere, local, local],
        out_specs=[local, local],
        scratch_shapes=[
            pltpu.VMEM((count, BLK_DEV, BLOCK * FEAT), jnp.bfloat16),
            pltpu.VMEM(selected.shape, jnp.int32),
            pltpu.SemaphoreType.DMA((count + 1,)),
        ],
        compiler_params=pltpu.CompilerParams(vmem_limit_bytes=46 * MIB),
        name="pick_blocks",
    )(selected, cache, packed, swapped)


def tie_kernel(*refs):
    pass


def tie(value, *earlier):
    anywhere = pl.BlockSpec(memory_space=pl.ANY)
    return pl.pallas_call(
        tie_kernel,
        out_shape=jax.ShapeDtypeStruct(value.shape, value.dtype),
        in_specs=[anywhere] * (1 + len(earlier)),
        out_specs=anywhere,
        input_output_aliases={0: 0},
        compiler_params=pltpu.CompilerParams(vmem_limit_bytes=MIB),
        name="tie",
    )(value, *earlier)


def spread_queries(packed):
    lane = lax.broadcasted_iota(jnp.int32, (RDEV * HEADS // 2, WIDE), 1)
    even = jnp.where(lane < FEAT, packed[:, :WIDE].astype(jnp.float32), 0.0)
    odd = jnp.where(lane >= KR, packed[:, KL:].astype(jnp.float32), 0.0)
    low = [even, pltpu.roll(odd, FEAT, 1)]
    high = [pltpu.roll(even, KR, 1), odd]
    return low, high


def attend_kernel(i, blocks_ref, selected_ref, _, *refs):
    width = GROUP * PAIRS
    pairs = jnp.concatenate(
        [blocks_ref[:, i, t].reshape(width, 128) for t in range(TILES)], axis=1
    )
    low, high = [], []
    views = [refs[0].at[0], refs[0].at[1]] if i else refs[:-1]
    for query_ref in views:
        parts = spread_queries(query_ref[...])
        low += parts[0]
        high += parts[1]
    query = jnp.concatenate(low, axis=0).astype(jnp.bfloat16)
    shifted = jnp.concatenate(high, axis=0).astype(jnp.bfloat16)
    out_ref = refs[-1]
    y, zhi, zlo, x, core = here()
    first, second = (owner_place(zhi, zlo, c, i) for c in range(2))
    pair = jnp.where(core == 0, first[0], second[0])
    chip = jnp.where(core == 0, first[1], second[1])
    owner = (y * NK + pair) * (2 * NX) + chip * NX + x
    slot = lax.broadcasted_iota(jnp.int32, (1, width), 1) >> 5
    holder = (slot & 3) * (NK * 2 * NX) + (zhi * (2 * NX) + ((slot >> 2) & 1) * NX + (slot >> 3))
    places = selected_ref[...] >> 3
    lane = lax.broadcasted_iota(jnp.int32, places.shape, 1)
    rows = []
    for j in range(RDEV):
        mine = jnp.sum(jnp.where(lane == RDEV * owner + j, places, 0), axis=1, keepdims=True)
        read = jnp.max(jnp.where(mine == holder, 1.0, 0.0), axis=0, keepdims=True)
        rows.append(jnp.broadcast_to(read, (HEADS // 2, width)))
    valid = jnp.concatenate(rows * 4, axis=0) > 0.5
    dims = (((1,), (1,)), ((), ()))
    odd_keys = pairs[:, KL:]
    even = lax.dot_general(query, pairs[:, :WIDE], dims, preferred_element_type=jnp.float32)
    odd = lax.dot_general(shifted, odd_keys, dims, preferred_element_type=jnp.float32)
    even = jnp.where(valid, even * score_scale, EMPTY)
    odd = jnp.where(valid, odd * score_scale, EMPTY)
    top = jnp.max(jnp.maximum(even, odd), axis=1, keepdims=True)
    even = jnp.exp(even - top)
    odd = jnp.exp(odd - top)
    total = jnp.sum(even + odd, axis=1, keepdims=True)
    value = jnp.dot(
        even.astype(jnp.bfloat16), pairs[:, :KL], preferred_element_type=jnp.float32
    )
    odd_value = jnp.dot(odd.astype(jnp.bfloat16), odd_keys, preferred_element_type=jnp.float32)
    value = (value + odd_value[:, KR : KR + KL]) * (1.0 / total)
    level = top + jnp.log(total)
    wide = jnp.transpose(jnp.broadcast_to(level, (2 * ROWS, 128)))[:TAIL]
    high = wide.astype(jnp.bfloat16).astype(jnp.float32)
    middle = (wide - high).astype(jnp.bfloat16).astype(jnp.float32)
    low = wide - high - middle
    line = lax.broadcasted_iota(jnp.int32, wide.shape, 0)
    tail = jnp.where(line == 0, high, jnp.where(line == 1, middle, jnp.where(line == 2, low, 0.0)))
    out_ref[: 2 * ROWS] = value.astype(jnp.bfloat16)
    out_ref[2 * ROWS :, : 2 * ROWS] = tail.astype(jnp.bfloat16)
    out_ref[2 * ROWS :, 2 * ROWS :] = jnp.zeros((TAIL, KL - 2 * ROWS), jnp.bfloat16)


def attend(i, blocks, selected, earlier, *queries):
    local = pl.BlockSpec(memory_space=pltpu.VMEM)
    return pl.pallas_call(
        functools.partial(attend_kernel, i),
        out_shape=jax.ShapeDtypeStruct((2 * ROWS + TAIL, KL), jnp.bfloat16),
        in_specs=[local, local, pl.BlockSpec(memory_space=pl.ANY)] + [local] * len(queries),
        out_specs=local,
        compiler_params=pltpu.CompilerParams(vmem_limit_bytes=24 * MIB),
        cost_estimate=pl.CostEstimate(flops=1, bytes_accessed=1, transcendentals=0),
        name="attend",
    )(blocks, selected, earlier, *queries)


def weigh(values, levels):
    peak = functools.reduce(jnp.maximum, levels)
    weights = [jnp.exp(level - peak) for level in levels]
    total = functools.reduce(jnp.add, weights)
    scale = 1.0 / total
    mean = jnp.zeros((ROWS, KL), jnp.float32)
    for value, weight in zip(values, weights):
        column = jnp.transpose(jnp.broadcast_to(weight * scale, (128, ROWS)))
        factor = jnp.concatenate([column] * (KL // 128), axis=1)
        mean = mean + factor * value.astype(jnp.float32)
    return mean, peak + jnp.log(total)


def halves_of(ref, half):
    tail = ref[2 * ROWS :, half * ROWS : (half + 1) * ROWS].astype(jnp.float32)
    return ref[half * ROWS : (half + 1) * ROWS], jnp.sum(tail, axis=0, keepdims=True)


def premerge_kernel(mine_ref, other_ref, out_ref):
    for half in range(2):
        views = [halves_of(mine_ref, half), halves_of(other_ref, 1 - half)]
        mean, level = weigh([view[0] for view in views], [view[1] for view in views])
        out_ref[half, :ROWS] = mean
        out_ref[half, ROWS:, :ROWS] = jnp.broadcast_to(level, (8, ROWS))
        out_ref[half, ROWS:, ROWS:] = jnp.zeros((8, KL - ROWS), jnp.float32)


def premerge(mine, other):
    return pl.pallas_call(
        premerge_kernel,
        out_shape=jax.ShapeDtypeStruct((2, ROWS + 8, KL), jnp.float32),
        compiler_params=pltpu.CompilerParams(vmem_limit_bytes=8 * MIB),
        name="premerge",
    )(mine, other)


def merge_kernel(state_ref, mine_ref, other_ref, out_ref):
    core = lax.axis_index("head")
    for half in range(2):
        state = (state_ref[half, :ROWS], state_ref[half, ROWS : ROWS + 1, :ROWS])
        views = [state, halves_of(mine_ref, half), halves_of(other_ref, 1 - half)]
        mean, _ = weigh([view[0] for view in views], [view[1] for view in views])
        mean = mean.reshape(2, RDEV, HEADS // 2, KL)
        for head in range(HEADS):
            pair, odd = head // 2, head % 2
            lines = [mean[odd, j, pair : pair + 1] for j in range(RDEV)]
            lane = pl.multiple_of((core ^ half) * HEADS * KL + head * KL, KL)
            out_ref[:, pl.ds(lane, KL)] = jnp.concatenate(lines, axis=0).astype(jnp.bfloat16)


def merge(parts):
    return pl.pallas_call(
        merge_kernel,
        out_shape=jax.ShapeDtypeStruct((RDEV, 2 * HEADS * KL), jnp.bfloat16),
        compiler_params=pltpu.CompilerParams(vmem_limit_bytes=12 * MIB),
        name="merge",
    )(*parts)


def per_device(queries, cache, selected):
    def move(value, i, back, cross):
        pairs = []
        for zz in range(NZ):
            for c in range(2):
                pair, chip = owner_place(zz // 2, zz % 2, c, i)
                pairs.append((zz * 2 + c, (pair * 2 + chip) * 2 + (c ^ cross)))
        pairs = [pair[::-1] for pair in pairs] if back else pairs
        return lax.ppermute(value, ("zhi", "zlo", "head"), pairs)

    swap = [(0, 1), (1, 0)]
    packed = queries.reshape(ROWS // 2, PAIR_WIDTH)
    asked = [[move(packed, 0, True, cross) for cross in range(2)]]
    picked, both = pick_blocks(selected.T, cache, packed, lax.ppermute(packed, "head", swap))
    picked = tie(picked, *asked[0])
    picked = picked.reshape(GROUP, COUNT * TILES * PAIRS, 128)
    blocks = lax.all_to_all(picked, ("x", "zlo", "y"), split_axis=0, concat_axis=0, tiled=True)
    blocks = blocks.reshape(GROUP, COUNT, TILES, PAIRS, 128)
    asked.append([move(tie(both, blocks), 1, True, 0)])

    mine, other, earlier = [], [], packed
    for i in range(COUNT):
        part = attend(i, blocks, selected.T, earlier, *asked[i])
        earlier = part
        mine.append(move(part, i, False, 0))
        other.append(lax.ppermute(mine[i], "head", swap))
    state = premerge(mine[0], other[0])
    return merge([state, mine[1], other[1]])


def solution(mesh):
    grid = Mesh(mesh.devices.reshape(NY, NK, 2, NX, 2), ("y", "zhi", "zlo", "x", "head"))
    seq = ("y", "zhi", "zlo", "x")
    placed = (P(seq, "head"), P(None, seq, None), P())
    return jax.shard_map(
        per_device, mesh=grid, in_specs=placed, out_specs=P(seq, None), check_vma=False
    )
```

```python
import functools

import jax
import jax.numpy as jnp
from jax import lax
from jax.experimental import pallas as pl
from jax.experimental.pallas import tpu as pltpu
from jax.sharding import Mesh
from jax.sharding import PartitionSpec as P

KL = 512
KR = 64
FEAT = KL + KR
WIDE = KL + 2 * KR
BLOCK = 64
PAIRS = BLOCK // 2
UNIT = PAIRS // 2
PAIR_WIDTH = 2 * FEAT
SPAN = UNIT * PAIR_WIDTH
TILES = PAIR_WIDTH // 128
TOPK = 32
RDEV = 2
BLK_DEV = 8
HEADS = 64
NY, NZ, NX = 4, 8, 4
NK = NZ // 2
GROUP = NY * 2 * NX
SEQ = NY * NZ * NX
ROWS = RDEV * HEADS
TAIL = 16
EMPTY = -1e30
MIB = 1024 * 1024

score_scale = 192.0 ** (-0.5)

COUNT = 2


def owner_place(zhi, zlo, core, i):
    if core == 0:
        return ((zhi + 2) % NK, 1 - zlo) if i == 0 else (zhi, zlo)
    return (zhi + 3 - 2 * zlo) % NK, zlo if i == 0 else 1 - zlo


def here():
    return tuple(lax.axis_index(name) for name in ("y", "zhi", "zlo", "x", "head"))


def pick_kernel(selected_ref, cache_ref, out_ref, held_ref, sems):
    steps = [(y, n) for y in range(NY) for n in range(COUNT)]
    y, zhi, zlo, x, core = here()
    pairs = [(zhi + jnp.where(core == 0, 2 - 2 * n, 3 - 2 * n)) % NK for n in range(COUNT)]

    def fetch(s):
        request = steps[s][0] * NK + pairs[steps[s][1]]
        return pltpu.make_async_copy(cache_ref.at[request], held_ref.at[s], sems.at[s])

    for s in range(len(steps)):
        fetch(s).start(priority=s % 2)
    me = ((y * NK + zhi) * 2 + zlo) * NX + x
    selected = selected_ref[...]
    inner = jnp.where((selected >> 3) == me, selected & (BLK_DEV - 1), -1)
    inner = jnp.max(inner, axis=0, keepdims=True)
    inner = jnp.maximum(inner, pltpu.roll(inner, SEQ * RDEV - 1, 1))
    row = lax.broadcasted_iota(jnp.int32, (2 * NX * UNIT, BLK_DEV * UNIT), 0)
    col = lax.broadcasted_iota(jnp.int32, (2 * NX * UNIT, BLK_DEV * UNIT), 1)
    token, held = (col >> 3) == (row & (UNIT - 1)), col & (BLK_DEV - 1)
    lane = lax.broadcasted_iota(jnp.int32, (2 * NX * UNIT, SEQ * RDEV), 1)
    slot = lax.broadcasted_iota(jnp.int32, (2 * NX * UNIT, SEQ * RDEV), 0) >> 4
    for s, (y, n) in enumerate(steps):
        base = (y * NK + pairs[n]) * (2 * NX)
        mine = lane == RDEV * (base + slot)
        block = jnp.sum(jnp.where(mine, inner, 0), axis=1, keepdims=True)
        onehot = jnp.where(token & (held == block), 1.0, 0.0).astype(jnp.bfloat16)
        fetch(s).wait()
        for half in range(2):
            pieces = [
                held_ref[s, :, p * PAIR_WIDTH : (p + 1) * PAIR_WIDTH].astype(jnp.float32)
                for p in range(half * UNIT, (half + 1) * UNIT)
            ]
            stacked = jnp.concatenate(pieces, axis=0).astype(jnp.bfloat16)
            picked = jnp.dot(onehot, stacked, preferred_element_type=jnp.float32)
            picked = picked.astype(jnp.bfloat16).reshape(2, NX, UNIT, PAIR_WIDTH)
            for zlo in range(2):
                chip = jnp.where(core == 0, 1 - zlo if n == 0 else zlo, n)
                index = jnp.where(core == 0, n, 0 if n == zlo else 1)
                span = slice(half * UNIT, (half + 1) * UNIT)
                for t in range(TILES):
                    tile = picked[zlo, :, :, t * 128 : (t + 1) * 128]
                    out_ref[:, chip, y, index, t, span] = tile


def pick_blocks(selected, cache):
    count = NY * COUNT
    return pl.pallas_call(
        pick_kernel,
        out_shape=jax.ShapeDtypeStruct((NX, 2, NY, COUNT, TILES, PAIRS, 128), jnp.bfloat16),
        in_specs=[pl.BlockSpec(memory_space=pltpu.VMEM), pl.BlockSpec(memory_space=pl.ANY)],
        out_specs=pl.BlockSpec(memory_space=pltpu.VMEM),
        scratch_shapes=[
            pltpu.VMEM((count, BLK_DEV, BLOCK * FEAT), jnp.bfloat16),
            pltpu.SemaphoreType.DMA((count,)),
        ],
        compiler_params=pltpu.CompilerParams(vmem_limit_bytes=46 * MIB),
        name="pick_blocks",
    )(selected, cache)


def tie_kernel(*refs):
    pass


def tie(value, *earlier):
    anywhere = pl.BlockSpec(memory_space=pl.ANY)
    return pl.pallas_call(
        tie_kernel,
        out_shape=jax.ShapeDtypeStruct(value.shape, value.dtype),
        in_specs=[anywhere] * (1 + len(earlier)),
        out_specs=anywhere,
        input_output_aliases={0: 0},
        compiler_params=pltpu.CompilerParams(vmem_limit_bytes=MIB),
        name="tie",
    )(value, *earlier)


def spread_queries(packed):
    lane = lax.broadcasted_iota(jnp.int32, (RDEV * HEADS // 2, WIDE), 1)
    even = jnp.where(lane < FEAT, packed[:, :WIDE].astype(jnp.float32), 0.0)
    odd = jnp.where(lane >= KR, packed[:, KL:].astype(jnp.float32), 0.0)
    low = [even, pltpu.roll(odd, FEAT, 1)]
    high = [pltpu.roll(even, KR, 1), odd]
    return low, high


def attend_kernel(i, blocks_ref, selected_ref, _, *refs):
    width = GROUP * PAIRS
    pairs = jnp.concatenate(
        [blocks_ref[:, i, t].reshape(width, 128) for t in range(TILES)], axis=1
    )
    low, high = [], []
    views = [refs[0].at[0], refs[0].at[1]] if i else refs[:-1]
    for query_ref in views:
        parts = spread_queries(query_ref[...])
        low += parts[0]
        high += parts[1]
    query = jnp.concatenate(low, axis=0).astype(jnp.bfloat16)
    shifted = jnp.concatenate(high, axis=0).astype(jnp.bfloat16)
    out_ref = refs[-1]
    y, zhi, zlo, x, core = here()
    first, second = (owner_place(zhi, zlo, c, i) for c in range(2))
    pair = jnp.where(core == 0, first[0], second[0])
    chip = jnp.where(core == 0, first[1], second[1])
    owner = (y * NK + pair) * (2 * NX) + chip * NX + x
    slot = lax.broadcasted_iota(jnp.int32, (1, width), 1) >> 5
    holder = (slot & 3) * (NK * 2 * NX) + (zhi * (2 * NX) + ((slot >> 2) & 1) * NX + (slot >> 3))
    places = selected_ref[...] >> 3
    lane = lax.broadcasted_iota(jnp.int32, places.shape, 1)
    rows = []
    for j in range(RDEV):
        mine = jnp.sum(jnp.where(lane == RDEV * owner + j, places, 0), axis=1, keepdims=True)
        read = jnp.max(jnp.where(mine == holder, 1.0, 0.0), axis=0, keepdims=True)
        rows.append(jnp.broadcast_to(read, (HEADS // 2, width)))
    valid = jnp.concatenate(rows * 4, axis=0) > 0.5
    dims = (((1,), (1,)), ((), ()))
    odd_keys = pairs[:, KL:]
    even = lax.dot_general(query, pairs[:, :WIDE], dims, preferred_element_type=jnp.float32)
    odd = lax.dot_general(shifted, odd_keys, dims, preferred_element_type=jnp.float32)
    even = jnp.where(valid, even * score_scale, EMPTY)
    odd = jnp.where(valid, odd * score_scale, EMPTY)
    top = jnp.max(jnp.maximum(even, odd), axis=1, keepdims=True)
    even = jnp.where(valid, jnp.exp(even - top), 0.0)
    odd = jnp.where(valid, jnp.exp(odd - top), 0.0)
    total = jnp.maximum(jnp.sum(even + odd, axis=1, keepdims=True), 1.0)
    value = jnp.dot(
        even.astype(jnp.bfloat16), pairs[:, :KL], preferred_element_type=jnp.float32
    )
    odd_value = jnp.dot(odd.astype(jnp.bfloat16), odd_keys, preferred_element_type=jnp.float32)
    value = (value + odd_value[:, KR : KR + KL]) * (1.0 / total)
    level = top + jnp.log(total)
    wide = jnp.transpose(jnp.broadcast_to(level, (2 * ROWS, 128)))[:TAIL]
    high = wide.astype(jnp.bfloat16).astype(jnp.float32)
    middle = (wide - high).astype(jnp.bfloat16).astype(jnp.float32)
    low = wide - high - middle
    line = lax.broadcasted_iota(jnp.int32, wide.shape, 0)
    tail = jnp.where(line == 0, high, jnp.where(line == 1, middle, jnp.where(line == 2, low, 0.0)))
    out_ref[: 2 * ROWS] = value.astype(jnp.bfloat16)
    out_ref[2 * ROWS :, : 2 * ROWS] = tail.astype(jnp.bfloat16)
    out_ref[2 * ROWS :, 2 * ROWS :] = jnp.zeros((TAIL, KL - 2 * ROWS), jnp.bfloat16)


def attend(i, blocks, selected, earlier, *queries):
    local = pl.BlockSpec(memory_space=pltpu.VMEM)
    return pl.pallas_call(
        functools.partial(attend_kernel, i),
        out_shape=jax.ShapeDtypeStruct((2 * ROWS + TAIL, KL), jnp.bfloat16),
        in_specs=[local, local, pl.BlockSpec(memory_space=pl.ANY)] + [local] * len(queries),
        out_specs=local,
        compiler_params=pltpu.CompilerParams(vmem_limit_bytes=24 * MIB),
        cost_estimate=pl.CostEstimate(flops=1, bytes_accessed=1, transcendentals=0),
        name="attend",
    )(blocks, selected, earlier, *queries)


def weigh(values, levels):
    peak = functools.reduce(jnp.maximum, levels)
    weights = [jnp.exp(level - peak) for level in levels]
    total = functools.reduce(jnp.add, weights)
    scale = 1.0 / total
    mean = jnp.zeros((ROWS, KL), jnp.float32)
    for value, weight in zip(values, weights):
        column = jnp.transpose(jnp.broadcast_to(weight * scale, (128, ROWS)))
        factor = jnp.concatenate([column] * (KL // 128), axis=1)
        mean = mean + factor * value.astype(jnp.float32)
    return mean, peak + jnp.log(total)


def halves_of(ref, half):
    tail = ref[2 * ROWS :, half * ROWS : (half + 1) * ROWS].astype(jnp.float32)
    return ref[half * ROWS : (half + 1) * ROWS], jnp.sum(tail, axis=0, keepdims=True)


def premerge_kernel(mine_ref, other_ref, out_ref):
    for half in range(2):
        views = [halves_of(mine_ref, half), halves_of(other_ref, 1 - half)]
        mean, level = weigh([view[0] for view in views], [view[1] for view in views])
        out_ref[half, :ROWS] = mean
        out_ref[half, ROWS:, :ROWS] = jnp.broadcast_to(level, (8, ROWS))
        out_ref[half, ROWS:, ROWS:] = jnp.zeros((8, KL - ROWS), jnp.float32)


def premerge(mine, other):
    return pl.pallas_call(
        premerge_kernel,
        out_shape=jax.ShapeDtypeStruct((2, ROWS + 8, KL), jnp.float32),
        compiler_params=pltpu.CompilerParams(vmem_limit_bytes=8 * MIB),
        name="premerge",
    )(mine, other)


def merge_kernel(state_ref, mine_ref, other_ref, out_ref):
    core = lax.axis_index("head")
    for half in range(2):
        state = (state_ref[half, :ROWS], state_ref[half, ROWS : ROWS + 1, :ROWS])
        views = [state, halves_of(mine_ref, half), halves_of(other_ref, 1 - half)]
        mean, _ = weigh([view[0] for view in views], [view[1] for view in views])
        mean = mean.astype(jnp.bfloat16).reshape(2, RDEV, HEADS // 2, KL)
        for odd in range(2):
            out_ref[:, core ^ half, :, odd * KL : (odd + 1) * KL] = mean[odd]


def merge(parts):
    return pl.pallas_call(
        merge_kernel,
        out_shape=jax.ShapeDtypeStruct((RDEV, 2, HEADS // 2, 2 * KL), jnp.bfloat16),
        compiler_params=pltpu.CompilerParams(vmem_limit_bytes=12 * MIB),
        name="merge",
    )(*parts)


def per_device(queries, cache, selected):
    def move(value, i, back, cross):
        pairs = []
        for zz in range(NZ):
            for c in range(2):
                pair, chip = owner_place(zz // 2, zz % 2, c, i)
                pairs.append((zz * 2 + c, (pair * 2 + chip) * 2 + (c ^ cross)))
        pairs = [pair[::-1] for pair in pairs] if back else pairs
        return lax.ppermute(value, ("zhi", "zlo", "head"), pairs)

    swap = [(0, 1), (1, 0)]
    packed = queries.reshape(ROWS // 2, PAIR_WIDTH)
    asked = [[move(packed, 0, True, cross) for cross in range(2)]]
    both = jnp.stack([packed, lax.ppermute(tie(packed, asked[0][0]), "head", swap)])
    picked = tie(pick_blocks(selected.T, cache), *asked[0], both)
    picked = picked.reshape(GROUP, COUNT * TILES * PAIRS, 128)
    blocks = lax.all_to_all(picked, ("x", "zlo", "y"), split_axis=0, concat_axis=0, tiled=True)
    blocks = blocks.reshape(GROUP, COUNT, TILES, PAIRS, 128)
    asked.append([move(tie(both, blocks), 1, True, 0)])

    mine, other, earlier = [], [], packed
    for i in range(COUNT):
        part = attend(i, blocks, selected.T, earlier, *asked[i])
        earlier = part
        mine.append(move(part, i, False, 0))
        other.append(lax.ppermute(mine[i], "head", swap))
    state = premerge(mine[0], other[0])
    return merge([state, mine[1], other[1]]).reshape(RDEV, 2 * HEADS * KL)


def solution(mesh):
    grid = Mesh(mesh.devices.reshape(NY, NK, 2, NX, 2), ("y", "zhi", "zlo", "x", "head"))
    seq = ("y", "zhi", "zlo", "x")
    placed = (P(seq, "head"), P(None, seq, None), P())
    return jax.shard_map(
        per_device, mesh=grid, in_specs=placed, out_specs=P(seq, None), check_vma=False
    )
```
